32 devices in a mesh: dp: 8 (over z, core), ctx: 4 (over y, x).
Axes of the slice: x: 2, y: 2, z: 4, core: 2. Of those that a mesh axis runs over, the one named last changes fastest.
Arguments:
- gene_ids: int32 [8, 512], P('dp', 'ctx'), may hold values from 0 to 9631, as said below
- counts: int32 [8, 512], P('dp', 'ctx'), may hold values from 1 to 1024
- values: float32 [8, 512], P('dp', 'ctx'), may hold values from -6 to 6
- lengths: int32 [8], P('dp'), may hold values from 1 to 512, 1365 in all
- bin_edges: int32 [8, 50], P('dp'), may hold values from 1 to 1024, as said below
- bin_table: bfloat16 [51, 384], replicated, may hold values from -6 to 6
- value_weight: float32 [384], replicated, may hold values from -6 to 6
- in_weight: bfloat16 [384, 2048], P(None, 'dp'), may hold values from -0.3125 to 0.3125
- out_weight: bfloat16 [2048, 384], P('dp'), may hold values from -0.125 to 0.125
- gene_table: bfloat16 [9632, 384], P('ctx'), may hold values from -6 to 6
- zero_embed: bfloat16 [384], replicated, may hold values from -6 to 6
- qkv_weight: bfloat16 [384, 1152], replicated, may hold values from -0.3125 to 0.3125
- proj_weight: bfloat16 [384, 384], replicated, may hold values from -0.3125 to 0.3125
- readout: float32 [384], replicated, may hold values from -0.3125 to 0.3125
- targets: float32 [8, 9632], P('dp', 'ctx'), may hold values from -6 to 6
Outputs:
- predicted: float32 [8, 9632], P('dp', 'ctx')
- grad_qkv: float32 [384, 1152], P('dp', 'ctx')
The draws below stay inside these ranges and needn't reach their ends.
Inputs may be any that keep to these rules, and one draw needn't show every extreme that they name: `gene_ids`: within one cell all entries are distinct. Of the 128 entries of one cell held by one index of ctx, exactly 32 lie in each block of 2408 consecutive genes. Entries at positions from the cell's length on are unused. `bin_edges`: strictly increasing along each row; the last edge of every cell is 1024. `lengths`: they sum to 1365 and the largest is 512.
All inputs are finite; a program needn't handle non-finite values. No bound on the sum of `lengths` on one device may be relied on, other than what follows from the above.
Results may differ from the reference program's by a relative error of at most 0.003.
The reference program's roundings to bfloat16 on the way (of `normed_tokens`, `activated`, `encoded`, `gene_input`, `normed`, `attended`, `hidden_grad` and `grad_rows`) count: a program that leaves them out, or rounds other values in their place, can miss the bound.
Values may be sent and summed in bfloat16 or wider, within the bound.
A program may use at most 128 MiB of HBM per device.

```python
import math
import jax
import jax.numpy as jnp
import numpy as np
from jax import lax

D = 384
HEAD = 64
HEADS = 6
FF = 2048
GENES = 9632
BINS = 51
EDGES = 50
TOK_DEV = 128
CELLS = 8
CELL_SLOTS = 512
GENE_DEV = 2408
CAP = 32


def draw_gene_ids(key, part):
    blocks = CELL_SLOTS // TOK_DEV
    slot_keys = jax.random.split(jax.random.fold_in(key, 11), CELLS * blocks)
    shuffles = jax.vmap(lambda one_key: jax.random.permutation(one_key, TOK_DEV))(slot_keys).astype(jnp.int32)
    ranges = shuffles // CAP
    ranks = shuffles % CAP
    gene_keys = jax.random.split(jax.random.fold_in(key, 12), CELLS * blocks)
    layouts = jax.vmap(lambda one_key: jax.random.permutation(one_key, GENE_DEV))(gene_keys).astype(jnp.int32)
    layouts = layouts.reshape(CELLS, blocks, GENE_DEV)
    flat_index = jnp.arange(CELLS * blocks, dtype=jnp.int32)
    source = (flat_index % blocks)[:, None]
    cell_index = (flat_index // blocks)[:, None]
    position = source * CAP + ranks
    within = layouts[cell_index, ranges, position]
    genes = ranges * GENE_DEV + within
    return genes.reshape(CELLS, CELL_SLOTS).astype(jnp.int32)


def draw_counts(key, part):
    exponents = jax.random.randint(jax.random.fold_in(key, 21), (CELLS, CELL_SLOTS), 1, 11)
    tops = jnp.left_shift(jnp.ones((CELLS, CELL_SLOTS), jnp.int32), exponents)
    return jax.random.randint(jax.random.fold_in(key, 22), (CELLS, CELL_SLOTS), 1, tops + 1).astype(jnp.int32)


def draw_bin_edges(key, part):
    edge_keys = jax.random.split(jax.random.fold_in(key, 31), CELLS)
    chosen = jax.vmap(lambda one_key: jax.random.permutation(one_key, 1023)[:EDGES - 1])(edge_keys).astype(jnp.int32) + 1
    ordered = jnp.sort(chosen, axis=1)
    last_edge = jnp.full((CELLS, 1), 1024, jnp.int32)
    return jnp.concatenate([ordered, last_edge], axis=1).astype(jnp.int32)


def levels(key, extent, pieces, least, top_value):
    def one(axis_at, shards_of):
        heights = jax.random.uniform(jax.random.fold_in(jax.random.fold_in(key, 6), axis_at), (shards_of,), jnp.float32, least / len(pieces), top_value / len(pieces))
        return jnp.repeat(jnp.exp(heights), extent[axis_at] // shards_of).reshape((-1,) + (1,) * (len(extent) - axis_at - 1))

    loudness = one(*pieces[0])
    for cut in pieces[1:]:
        loudness = loudness * one(*cut)
    return loudness


def length_profile(count, total, limit, lean):
    loads = [(1 << 20) // math.isqrt(grade ** lean) + 1 for grade in range(2, count + 1)]
    surplus, holding = total - limit - (count - 1), [1] * (count - 1)
    while surplus > 0:
        movable = [i for i in range(count - 1) if holding[i] < limit]
        whole, budget = sum([loads[i] for i in movable]), surplus
        for i in movable:
            more = min(limit - holding[i], max(1, budget * loads[i] // whole), surplus)
            holding[i] = holding[i] + more
            surplus = surplus - more
    return np.array([limit] + holding)


def ragged_sizes(stream_key, amount, total, most, skew):
    if amount == 2:
        one = jax.random.randint(stream_key, (), max(1, total - most), min(most, total - 1) + 1)
        return jnp.stack([one, total - one])
    tallies = jnp.asarray(length_profile(amount, total, most, skew), jnp.int32)
    pairs = (amount - 1) // 2
    donor, sink = tallies[1:1 + 2 * pairs:2], tallies[2:2 + 2 * pairs:2]
    slack = jnp.minimum(donor - 1, most - sink)
    passed = jax.random.randint(jax.random.fold_in(stream_key, 1), (pairs,), 0, 1 << 20) % (slack + 1)
    tallies = tallies.at[1:1 + 2 * pairs:2].set(donor - passed).at[2:2 + 2 * pairs:2].set(sink + passed)
    return tallies[jax.random.permutation(jax.random.fold_in(stream_key, 2), amount)]


def scatter_about(stream_key, dims, scale, bound, pieces=(), kind=jnp.bfloat16):
    result = jax.random.normal(stream_key, dims, jnp.float32) * scale
    if len(pieces) > 0:
        result = levels(stream_key, dims, pieces, -0.22, 0.18) * result
    return jnp.clip(result, min=-bound, max=bound).astype(kind)


def setup_inputs(seed: int = 0) -> dict:
    key_list = jax.random.split(jax.random.key(seed), 16)
    gene_ids = draw_gene_ids(jax.random.fold_in(key_list[15], 71), 0)
    counts = draw_counts(jax.random.fold_in(key_list[15], 71), 0)
    values = scatter_about(key_list[2], (CELLS, CELL_SLOTS), 1.0, 6.0, ((0, 8), (1, 4)), jnp.float32)
    lengths = ragged_sizes(key_list[3], CELLS, CELLS * CELL_SLOTS // 3, CELL_SLOTS, 2).astype(jnp.int32)
    bin_edges = draw_bin_edges(jax.random.fold_in(key_list[15], 71), 0)
    bin_table = scatter_about(key_list[5], (BINS, D), 1.0, 6.0)
    value_weight = scatter_about(key_list[6], (D,), 1.0, 6.0, (), jnp.float32)
    in_weight = scatter_about(key_list[7], (D, FF), D ** -0.5, 0.3125, ((1, 8),))
    out_weight = scatter_about(key_list[8], (FF, D), FF ** -0.5, 0.125, ((0, 8),))
    gene_table = scatter_about(key_list[9], (GENES, D), 1.0, 6.0, ((0, 4),))
    zero_embed = scatter_about(key_list[10], (D,), 1.0, 6.0)
    qkv_weight = scatter_about(key_list[11], (D, 3 * D), D ** -0.5, 0.3125)
    proj_weight = scatter_about(key_list[12], (D, D), D ** -0.5, 0.3125)
    readout = scatter_about(key_list[13], (D,), D ** -0.5, 0.3125, (), jnp.float32)
    targets = scatter_about(key_list[14], (CELLS, GENES), 1.0, 6.0, ((0, 8), (1, 4)), jnp.float32)
    return dict(gene_ids=gene_ids, counts=counts, values=values, lengths=lengths, bin_edges=bin_edges, bin_table=bin_table, value_weight=value_weight, in_weight=in_weight, out_weight=out_weight, gene_table=gene_table, zero_embed=zero_embed, qkv_weight=qkv_weight, proj_weight=proj_weight, readout=readout, targets=targets)


feature_scale = 2.5
norm_eps = 1e-06
highest = lax.Precision.HIGHEST

def featurize(projected):
    inverse = lax.rsqrt(lax.optimization_barrier(jnp.mean(projected * projected, axis=-1, keepdims=True)) + norm_eps)
    return jnp.exp(feature_scale * projected * inverse)

def rms_round(matrix):
    inverse = lax.rsqrt(lax.optimization_barrier(jnp.mean(matrix * matrix, axis=-1, keepdims=True)) + norm_eps)
    return (matrix * inverse).astype(jnp.bfloat16)

def embed_tokens(token_counts, token_values, cell_edges, bin_table, value_weight):
    binned = lax.optimization_barrier(jnp.sum((token_counts[:, None] >= cell_edges[None, :]).astype(jnp.int32), axis=1))
    one_hot = (binned[:, None] == jnp.arange(bin_table.shape[0], dtype=jnp.int32)[None, :]).astype(jnp.bfloat16)
    looked = jnp.dot(one_hot, bin_table, preferred_element_type=jnp.float32)
    return looked + token_values[:, None] * value_weight[None, :]

def encode(token_counts, token_values, cell_edges, bin_table, value_weight, in_weight, out_weight):
    embedded = embed_tokens(token_counts, token_values, cell_edges, bin_table, value_weight)
    normed_tokens = rms_round(embedded)
    activated = jax.nn.silu(jnp.dot(normed_tokens, in_weight, preferred_element_type=jnp.float32)).astype(jnp.bfloat16)
    return (embedded + jnp.dot(activated, out_weight, preferred_element_type=jnp.float32)).astype(jnp.bfloat16)

def assemble(gene_rows, local_index, arrived, zero_embed):
    row_count = gene_rows.shape[0]
    placed = jnp.zeros((row_count, gene_rows.shape[1]), jnp.float32).at[local_index].set(arrived.astype(jnp.float32), mode='drop')
    marked = jnp.zeros((row_count,), jnp.int32).at[local_index].set(1, mode='drop')
    filled = jnp.where(marked[:, None] == 1, placed, zero_embed.astype(jnp.float32)[None, :])
    return (gene_rows.astype(jnp.float32) + filled).astype(jnp.bfloat16)

def project_heads(normed, qkv_weight):
    projected = jnp.dot(normed, qkv_weight, preferred_element_type=jnp.float32)
    row_count = projected.shape[0]
    model_width = qkv_weight.shape[0]
    query_raw = projected[:, :model_width].reshape(row_count, HEADS, HEAD)
    key_raw = projected[:, model_width:2 * model_width].reshape(row_count, HEADS, HEAD)
    value_raw = projected[:, 2 * model_width:].reshape(row_count, HEADS, HEAD)
    return (query_raw, key_raw, value_raw)

def summarize(key_feat, value_raw):
    summary = jnp.einsum('ghj,ghe->hje', key_feat, value_raw, precision=highest)
    return (summary, lax.optimization_barrier(jnp.sum(key_feat, axis=0)))

def attend(query_feat, summary, key_total):
    numerator = jnp.einsum('ghj,hje->ghe', query_feat, summary, precision=highest)
    denominator = jnp.einsum('ghj,hj->gh', query_feat, key_total, precision=highest)
    return (numerator / denominator[..., None], denominator)

def readout_pass(gene_input, attention, proj_weight, readout):
    attended = attention.reshape(attention.shape[0], -1).astype(jnp.bfloat16)
    hidden_out = gene_input.astype(jnp.float32) + jnp.dot(attended, proj_weight, preferred_element_type=jnp.float32)
    return lax.optimization_barrier(jnp.sum(hidden_out * readout[None, :], axis=1))

def back_to_attention(residual_grad, readout, proj_weight):
    hidden_grad = (residual_grad[:, None] * readout[None, :]).astype(jnp.bfloat16)
    grad_attn = lax.dot_general(hidden_grad, proj_weight, (((1,), (1,)), ((), ())), preferred_element_type=jnp.float32)
    return grad_attn.reshape(grad_attn.shape[0], HEADS, HEAD)

def attention_grads(grad_attn, attention, denominator, summary, key_total, query_feat):
    grad_numer = grad_attn / denominator[..., None]
    grad_denom = -lax.optimization_barrier(jnp.sum(grad_attn * attention, axis=-1)) / denominator
    grad_qfeat = jnp.einsum('ghe,hje->ghj', grad_numer, summary, precision=highest) + grad_denom[..., None] * key_total[None]
    part_summary = jnp.einsum('ghj,ghe->hje', query_feat, grad_numer, precision=highest)
    part_total = jnp.einsum('ghj,gh->hj', query_feat, grad_denom, precision=highest)
    return (grad_qfeat, part_summary, part_total)

def key_value_grads(grad_summary, grad_total, key_feat, value_raw):
    grad_kfeat = jnp.einsum('ghe,hje->ghj', value_raw, grad_summary, precision=highest) + grad_total[None]
    grad_value = jnp.einsum('ghj,hje->ghe', key_feat, grad_summary, precision=highest)
    return (grad_kfeat, grad_value)

def input_grads(query_raw, key_raw, grad_qfeat, grad_kfeat, grad_value):
    row_count = query_raw.shape[0]
    grad_query = jax.vjp(featurize, query_raw)[1](grad_qfeat)[0]
    grad_key = jax.vjp(featurize, key_raw)[1](grad_kfeat)[0]
    joined = jnp.concatenate([grad_query.reshape(row_count, -1), grad_key.reshape(row_count, -1), grad_value.reshape(row_count, -1)], axis=1)
    return joined.astype(jnp.bfloat16)

def reference(gene_ids, counts, values, lengths, bin_edges, bin_table, value_weight, in_weight, out_weight, gene_table, zero_embed, qkv_weight, proj_weight, readout, targets):
    grad_scale = 1.0 / math.sqrt(GENES * CELLS)

    def cell_step(grad_sum, cell):
        gene_row, count_row, value_row, length, cell_edges, target_row = cell
        encoded = encode(count_row, value_row, cell_edges, bin_table, value_weight, in_weight, out_weight)
        live_slot = jnp.arange(gene_row.shape[0], dtype=jnp.int32) < length
        local_index = jnp.where(live_slot, gene_row, GENES).astype(jnp.int32)
        gene_input = assemble(gene_table, local_index, encoded, zero_embed)
        normed = rms_round(gene_input.astype(jnp.float32))
        query_raw, key_raw, value_raw = project_heads(normed, qkv_weight)
        query_feat = featurize(query_raw)
        key_feat = featurize(key_raw)
        summary, key_total = summarize(key_feat, value_raw)
        attention, denominator = attend(query_feat, summary, key_total)
        predicted = readout_pass(gene_input, attention, proj_weight, readout)
        residual_grad = (predicted - target_row) * grad_scale
        grad_attn = back_to_attention(residual_grad, readout, proj_weight)
        grad_qfeat, grad_summary, grad_total = attention_grads(grad_attn, attention, denominator, summary, key_total, query_feat)
        grad_kfeat, grad_value = key_value_grads(grad_summary, grad_total, key_feat, value_raw)
        grad_rows = input_grads(query_raw, key_raw, grad_qfeat, grad_kfeat, grad_value)
        grad_sum = grad_sum + lax.dot_general(normed, grad_rows, (((0,), (0,)), ((), ())), preferred_element_type=jnp.float32)
        return (grad_sum, predicted)
    start_grad = jnp.zeros((qkv_weight.shape[0], qkv_weight.shape[1]), jnp.float32)
    grad_qkv, predicted = lax.scan(cell_step, start_grad, (gene_ids, counts, values, lengths, bin_edges, targets))
    return (predicted, grad_qkv)
```

```python
import functools
import math

import jax
import jax.numpy as jnp
from jax import lax
from jax.experimental import pallas as pl
from jax.experimental.pallas import tpu as pltpu
from jax.sharding import PartitionSpec as P

HEAD = 64
HEADS = 6
CHUNKS = 8


feature_scale = 2.5
norm_eps = 1e-06
highest = lax.Precision.HIGHEST


def featurize(projected):
    inverse = lax.rsqrt(jnp.mean(projected * projected, axis=-1, keepdims=True) + norm_eps)
    return jnp.exp(feature_scale * projected * inverse)


def rms_round(matrix):
    inverse = lax.rsqrt(jnp.mean(matrix * matrix, axis=-1, keepdims=True) + norm_eps)
    return (matrix * inverse).astype(jnp.bfloat16)


def embed_tokens(token_counts, token_values, cell_edges, bin_table, value_weight):
    binned = jnp.sum((token_counts[:, None] >= cell_edges[None, :]).astype(jnp.int32), axis=1)
    one_hot = (binned[:, None] == jnp.arange(bin_table.shape[0], dtype=jnp.int32)[None, :]).astype(
        jnp.bfloat16
    )
    looked = jnp.dot(one_hot, bin_table, preferred_element_type=jnp.float32)
    return looked + token_values[:, None] * value_weight[None, :]


def encode(token_counts, token_values, cell_edges, bin_table, value_weight, in_weight, out_weight):
    embedded = embed_tokens(token_counts, token_values, cell_edges, bin_table, value_weight)
    normed_tokens = rms_round(embedded)
    activated = jax.nn.silu(
        jnp.dot(
            normed_tokens,
            lax.all_gather(in_weight, "dp", axis=1, tiled=True),
            preferred_element_type=jnp.float32,
        )
    ).astype(jnp.bfloat16)
    mixed = embedded + jnp.dot(
        activated,
        lax.all_gather(out_weight, "dp", axis=0, tiled=True),
        preferred_element_type=jnp.float32,
    )
    return mixed.astype(jnp.bfloat16)


def assemble(gene_rows, local_index, arrived, zero_embed):
    row_count = gene_rows.shape[0]
    placed = (
        jnp.zeros((row_count, gene_rows.shape[1]), jnp.float32)
        .at[local_index]
        .set(arrived.astype(jnp.float32), mode="drop")
    )
    marked = jnp.zeros((row_count,), jnp.int32).at[local_index].set(1, mode="drop")
    filled = jnp.where(marked[:, None] == 1, placed, zero_embed.astype(jnp.float32)[None, :])
    return (gene_rows.astype(jnp.float32) + filled).astype(jnp.bfloat16)


def project_heads(normed, qkv_weight):
    projected = jnp.dot(normed, qkv_weight, preferred_element_type=jnp.float32)
    row_count = projected.shape[0]
    model_width = qkv_weight.shape[0]
    query_raw = projected[:, :model_width].reshape(row_count, HEADS, HEAD)
    key_raw = projected[:, model_width : 2 * model_width].reshape(row_count, HEADS, HEAD)
    value_raw = projected[:, 2 * model_width :].reshape(row_count, HEADS, HEAD)
    return (query_raw, key_raw, value_raw)


def summarize(key_feat, value_raw):
    summary = jnp.einsum("ghj,ghe->hje", key_feat, value_raw, precision=highest)
    return (summary, jnp.sum(key_feat, axis=0))


def attend(query_feat, summary, key_total):
    numerator = jnp.einsum("ghj,hje->ghe", query_feat, summary, precision=highest)
    denominator = jnp.einsum("ghj,hj->gh", query_feat, key_total, precision=highest)
    return (numerator / denominator[..., None], denominator)


def readout_pass(gene_input, attention, proj_weight, readout):
    attended = attention.reshape(attention.shape[0], -1).astype(jnp.bfloat16)
    hidden_out = gene_input.astype(jnp.float32) + jnp.dot(
        attended, proj_weight, preferred_element_type=jnp.float32
    )
    return jnp.sum(hidden_out * readout[None, :], axis=1)


def back_to_attention(residual_grad, readout, proj_weight):
    hidden_grad = (residual_grad[:, None] * readout[None, :]).astype(jnp.bfloat16)
    grad_attn = lax.dot_general(
        hidden_grad, proj_weight, (((1,), (1,)), ((), ())), preferred_element_type=jnp.float32
    )
    return grad_attn.reshape(grad_attn.shape[0], HEADS, HEAD)


def attention_grads(grad_attn, attention, denominator, summary, key_total, query_feat):
    grad_numer = grad_attn / denominator[..., None]
    grad_denom = -jnp.sum(grad_attn * attention, axis=-1) / denominator
    grad_qfeat = (
        jnp.einsum("ghe,hje->ghj", grad_numer, summary, precision=highest)
        + grad_denom[..., None] * key_total[None]
    )
    part_summary = jnp.einsum("ghj,ghe->hje", query_feat, grad_numer, precision=highest)
    part_total = jnp.einsum("ghj,gh->hj", query_feat, grad_denom, precision=highest)
    return (grad_qfeat, part_summary, part_total)


def key_value_grads(grad_summary, grad_total, key_feat, value_raw):
    grad_kfeat = (
        jnp.einsum("ghe,hje->ghj", value_raw, grad_summary, precision=highest) + grad_total[None]
    )
    grad_value = jnp.einsum("ghj,hje->ghe", key_feat, grad_summary, precision=highest)
    return (grad_kfeat, grad_value)


def input_grads(query_raw, key_raw, grad_qfeat, grad_kfeat, grad_value):
    row_count = query_raw.shape[0]
    grad_query = jax.vjp(featurize, query_raw)[1](grad_qfeat)[0]
    grad_key = jax.vjp(featurize, key_raw)[1](grad_kfeat)[0]
    joined = jnp.concatenate(
        [
            grad_query.reshape(row_count, -1),
            grad_key.reshape(row_count, -1),
            grad_value.reshape(row_count, -1),
        ],
        axis=1,
    )
    return joined.astype(jnp.bfloat16)


def body(
    gene_ids,
    counts,
    values,
    lengths,
    bin_edges,
    bin_table,
    value_weight,
    in_weight,
    out_weight,
    gene_table,
    zero_embed,
    qkv_weight,
    proj_weight,
    readout,
    targets,
):
    ctx_count = lax.axis_size("ctx")
    slot_count = gene_ids.shape[1]
    gene_count = gene_table.shape[0]
    capacity = slot_count // ctx_count
    position = lax.axis_index("ctx") * slot_count + jnp.arange(slot_count, dtype=jnp.int32)
    live_slot = position < lengths[0]
    gene_row = gene_ids[0]
    target_range = gene_row // gene_count
    sort_order = jnp.argsort(target_range, stable=True)
    local_offset = jnp.where(live_slot, gene_row - target_range * gene_count, gene_count)[
        sort_order
    ]
    cell_edges = bin_edges[0]
    packed = jnp.stack([counts[0][sort_order], local_offset], axis=0).reshape(
        2, ctx_count, capacity
    )
    moved_values, moved_ints = (
        lax.all_to_all(
            values[0][sort_order].reshape(1, ctx_count, capacity),
            "ctx",
            split_axis=1,
            concat_axis=1,
            tiled=True,
        ),
        lax.all_to_all(packed, "ctx", split_axis=1, concat_axis=1, tiled=True),
    )
    arrived_index = moved_ints[1].reshape(slot_count)
    arrived = encode(
        moved_ints[0].reshape(slot_count),
        moved_values.reshape(slot_count),
        cell_edges,
        bin_table,
        value_weight,
        in_weight,
        out_weight,
    )
    gene_input = assemble(gene_table, arrived_index, arrived, zero_embed)
    normed = rms_round(gene_input.astype(jnp.float32))
    query_raw, key_raw, value_raw = project_heads(normed, qkv_weight)
    query_feat = featurize(query_raw)
    key_feat = featurize(key_raw)
    part_summary, part_total = summarize(key_feat, value_raw)
    summary, key_total = lax.psum((part_summary, part_total), "ctx")
    attention, denominator = attend(query_feat, summary, key_total)
    predicted = readout_pass(gene_input, attention, proj_weight, readout)
    grad_scale = 1.0 / math.sqrt(gene_count * ctx_count * lax.axis_size("dp"))
    residual_grad = (predicted - targets[0]) * grad_scale
    grad_attn = back_to_attention(residual_grad, readout, proj_weight)
    grad_qfeat, part_gsummary, part_gtotal = attention_grads(
        grad_attn, attention, denominator, summary, key_total, query_feat
    )
    grad_summary, grad_total = lax.psum((part_gsummary, part_gtotal), "ctx")
    grad_kfeat, grad_value = key_value_grads(grad_summary, grad_total, key_feat, value_raw)
    grad_rows = input_grads(query_raw, key_raw, grad_qfeat, grad_kfeat, grad_value)
    row_share = lax.psum_scatter(
        lax.dot_general(
            normed, grad_rows, (((0,), (0,)), ((), ())), preferred_element_type=jnp.float32
        ),
        "dp",
        scatter_dimension=0,
        tiled=True,
    )
    grad_qkv = lax.psum_scatter(row_share, "ctx", scatter_dimension=1, tiled=True)
    return (predicted[None, :], grad_qkv)


MESH = pl.DeviceIdType.MESH
F32 = jnp.float32
BF16 = jnp.bfloat16


def mm(left, right):
    return jnp.dot(left, right, preferred_element_type=F32)


def split(x):
    high = x.astype(BF16)
    return high, (x - high.astype(F32)).astype(BF16)


def head_sum(x, ones):
    high, low = split(x)
    parts = []
    for start in range(0, x.shape[1], 256):
        width = min(256, x.shape[1] - start)
        block = ones[:width, :width]
        parts.append(
            mm(high[:, start : start + width], block) + mm(low[:, start : start + width], block)
        )
    return jnp.concatenate(parts, axis=1)


def rms(x):
    return x * lax.rsqrt(jnp.mean(x * x, axis=-1, keepdims=True) + norm_eps)


def lanes_to_rows(row, rows=128):
    return jnp.transpose(jnp.broadcast_to(row, (rows, row.shape[1])))


def send(src, dst, sems, index_send, index_recv, device):
    copy = pltpu.make_async_remote_copy(
        src_ref=src,
        dst_ref=dst,
        send_sem=sems[0].at[index_send],
        recv_sem=sems[1].at[index_recv],
        device_id=device,
        device_id_type=MESH,
    )
    copy.start()
    return copy


def kernel(
    gene_count,
    chunk,
    ids_ref,
    counts_ref,
    values_ref,
    lengths_ref,
    edges_ref,
    table_ref,
    vweight_ref,
    in_ref,
    out_ref,
    gene_ref,
    zero_ref,
    qkv_ref,
    proj_ref,
    readout_ref,
    targets_ref,
    pred_ref,
    grad_ref,
    table,
    ones,
    wvw_hi,
    wvw_lo,
    slots,
    tokens,
    ff_send,
    ff_recv,
    normed,
    unit,
    inverse,
    vwx,
    rows,
    base_dot,
    target_x,
    keep_x,
    pred_x,
    sums1,
    sums2,
    grads,
    core_recv,
    z_send,
    z_recv,
    part,
    ctx_recv,
    slot_s,
    slot_r,
    tok_s,
    tok_r,
    ff_s,
    ff_r,
    one_s,
    one_r,
    two_s,
    two_r,
    core_s,
    core_r,
    z_s,
    z_r,
    last_s,
    last_r,
):
    ctx = lax.axis_index("ctx")
    dp = lax.axis_index("dp")
    ctx_n = slots.shape[0]
    dp_n = tokens.shape[0]
    padded = gene_ref.shape[0]
    width = gene_ref.shape[1]
    tok_n = ids_ref.shape[1]
    cap = tok_n // ctx_n

    barrier = pltpu.get_barrier_semaphore()
    for k in range(1, ctx_n):
        pl.semaphore_signal(
            barrier, inc=1, device_id={"ctx": lax.rem(ctx + k, ctx_n)}, device_id_type=MESH
        )
    for k in range(1, dp_n):
        pl.semaphore_signal(
            barrier, inc=1, device_id={"dp": lax.rem(dp + k, dp_n)}, device_id_type=MESH
        )

    counts = counts_ref[...]
    binned = jnp.zeros(counts.shape, F32)
    for j in range(edges_ref.shape[1]):
        binned = binned + jnp.where(counts >= edges_ref[0, j], 1.0, 0.0)
    lane = lax.broadcasted_iota(jnp.int32, (1, tok_n), 1)
    live = (ctx * tok_n + lane) < lengths_ref[0]
    gene_f = jnp.where(live, ids_ref[...].astype(F32), -1.0)
    sub = lax.broadcasted_iota(jnp.int32, (8, tok_n), 0)
    slots[ctx] = jnp.where(
        sub == 0, gene_f, jnp.where(sub == 1, binned, jnp.where(sub == 2, values_ref[...], 0.0))
    )
    pl.semaphore_wait(barrier, ctx_n + dp_n - 2)
    copies = []
    for k in range(1, ctx_n):
        copies.append(
            send(
                slots.at[ctx],
                slots.at[ctx],
                (slot_s, slot_r),
                k,
                k,
                {"ctx": lax.rem(ctx + k, ctx_n)},
            )
        )

    hrow = lax.broadcasted_iota(jnp.int32, (256, 256), 0) // HEAD
    hcol = lax.broadcasted_iota(jnp.int32, (256, 256), 1) // HEAD
    ones[...] = jnp.where(hrow == hcol, 1.0, 0.0).astype(BF16)
    readout = readout_ref[...]
    w_col = jnp.sum(proj_ref[...].astype(F32) * readout, axis=1, keepdims=True)
    w_row = jnp.transpose(jnp.broadcast_to(w_col, (width, 128)))[0:1, :]
    v_dot = head_sum(qkv_ref[:, 2 * width :].astype(F32) * w_row, ones)
    v_high, v_low = split(v_dot)
    wvw_hi[...] = v_high
    wvw_lo[...] = v_low
    table[...] = jnp.zeros_like(table)
    table[0 : table_ref.shape[0], :] = table_ref[...].astype(F32)
    table_b = table[...].astype(BF16)
    target_x[0:padded, :] = lanes_to_rows(targets_ref[...])
    for copy in copies:
        copy.wait()

    first = (ctx * gene_count).astype(F32)
    upper = jnp.where(
        lax.broadcasted_iota(jnp.int32, (tok_n, tok_n), 0)
        < lax.broadcasted_iota(jnp.int32, (tok_n, tok_n), 1),
        1.0,
        0.0,
    ).astype(BF16)
    place = lax.broadcasted_iota(jnp.int32, (cap, tok_n), 0).astype(F32)
    idx_parts, bin_parts, val_parts = [], [], []
    for s in range(ctx_n):
        held = slots[s]
        local = held - first
        inside = (held >= first) & (local < gene_count)
        inside = jnp.where(inside, 1.0, 0.0)
        rank = mm(inside.astype(BF16), upper)
        chosen = (inside[0:1] > 0.5) & (rank[0:1] == place)
        idx_parts.append(jnp.sum(jnp.where(chosen, local[0:1] + 1.0, 0.0), axis=1, keepdims=True))
        bin_parts.append(jnp.sum(jnp.where(chosen, held[1:2], 0.0), axis=1, keepdims=True))
        val_parts.append(jnp.sum(jnp.where(chosen, held[2:3], 0.0), axis=1, keepdims=True))
    idx_col = jnp.concatenate(idx_parts, axis=0) - 1.0
    bin_col = jnp.concatenate(bin_parts, axis=0)
    val_col = jnp.concatenate(val_parts, axis=0)
    square = lax.broadcasted_iota(jnp.int32, (tok_n, 128), 1)
    mine = jnp.transpose(
        jnp.where(square == 0, bin_col, jnp.where(square == 1, val_col, jnp.where(square == 2, idx_col, 0.0)))
    )
    tokens[dp] = mine[0:8]
    copies = []
    for k in range(1, dp_n):
        copies.append(
            send(
                tokens.at[dp], tokens.at[dp], (tok_s, tok_r), k, k, {"dp": lax.rem(dp + k, dp_n)}
            )
        )
    idx_row = mine[2:3]

    gene_lane = lax.broadcasted_iota(jnp.int32, (tok_n, padded), 1).astype(F32)
    hit = gene_lane == idx_col
    token_base = mm(jnp.where(hit, 1.0, 0.0).astype(BF16), gene_ref[...])
    taken = jnp.sum(jnp.where(hit, 1.0, 0.0), axis=0, keepdims=True)
    tok_target = jnp.sum(jnp.where(hit, targets_ref[...], 0.0), axis=1, keepdims=True)
    in_range = lax.broadcasted_iota(jnp.int32, (1, padded), 1) < gene_count
    keep_row = jnp.where(in_range & (taken < 0.5), 1.0, 0.0)
    keep_x[0:padded, :] = lanes_to_rows(keep_row)
    tok_live = jnp.where(idx_col > -0.5, 1.0, 0.0)
    keep_x[padded:, :] = jnp.broadcast_to(tok_live, (tok_n, 128))
    target_x[padded:, :] = jnp.broadcast_to(tok_target, (tok_n, 128))

    pick = lax.broadcasted_iota(jnp.int32, (tok_n, table.shape[0]), 1).astype(F32)

    def embed(bin_c, val_c):
        one_hot = jnp.where(bin_c == pick, 1.0, 0.0).astype(BF16)
        return mm(one_hot, table_b) + val_c * vweight_ref[...]

    def feed(emb):
        pre = mm(rms(emb).astype(BF16), in_ref[...])
        act = (pre / (1.0 + jnp.exp(-pre))).astype(BF16)
        return mm(act, out_ref[...])

    ff_copies = []
    for k in range(1, dp_n):
        copies[k - 1].wait()
    for k in range(1, dp_n):
        other = lax.rem(dp + k, dp_n)
        got = jnp.transpose(jnp.concatenate([tokens[other]] * (128 // 8), axis=0))
        ff_send[k] = feed(embed(got[:, 0:1], got[:, 1:2])).astype(BF16)
        ff_copies.append(
            send(ff_send.at[k], ff_recv.at[k], (ff_s, ff_r), k, k, {"dp": other})
        )
    own_emb = embed(bin_col, val_col)
    own_mix = own_emb + feed(own_emb)

    def features(start, count, gene_input):
        at = pl.ds(start, count)
        gi = gene_input.astype(BF16).astype(F32)
        nb = rms(gi).astype(BF16)
        normed[at, :] = nb
        base_dot[at, :] = jnp.broadcast_to(
            jnp.sum(gi * readout, axis=1, keepdims=True), (count, 128)
        )
        raw = mm(nb, qkv_ref[:, : 2 * width])
        inv = lax.rsqrt(head_sum(raw * raw, ones) * (1.0 / HEAD) + norm_eps)
        u = raw * inv
        unit[at, :] = u
        inverse[at, :] = inv
        vw = mm(nb, wvw_hi[...]) + mm(nb, wvw_lo[...])
        vwx[at, :] = vw
        kf = jnp.exp(feature_scale * u[:, width:]) * keep_x[at, 0:1]
        return (
            jnp.sum(kf, axis=0, keepdims=True),
            jnp.sum(kf * vw, axis=0, keepdims=True),
        )

    zero = zero_ref[...].astype(F32)
    none = jnp.zeros((1, width), F32)

    def first_pass(i, carry):
        start = pl.multiple_of(i * chunk, 16)
        a, b = features(start, chunk, gene_ref[pl.ds(start, chunk), :].astype(F32) + zero)
        return carry[0] + a, carry[1] + b

    kt, us = lax.fori_loop(0, padded // chunk, first_pass, (none, none))
    for copy in ff_copies:
        copy.wait()
    for k in range(1, dp_n):
        own_mix = own_mix + ff_recv[k].astype(F32)
    a, b = features(padded, tok_n, token_base + own_mix.astype(BF16).astype(F32))
    kt, us = kt + a, us + b

    def over_ctx(buffer, sems, x, y):
        row_at = lax.broadcasted_iota(jnp.int32, (8, width), 0)
        buffer[ctx] = jnp.where(row_at == 0, x, jnp.where(row_at == 1, y, 0.0))
        sent = []
        for k in range(1, ctx_n):
            sent.append(
                send(buffer.at[ctx], buffer.at[ctx], sems, k, k, {"ctx": lax.rem(ctx + k, ctx_n)})
            )
        for copy in sent:
            copy.wait()
        total = buffer[0]
        for s in range(1, ctx_n):
            total = total + buffer[s]
        return total[0:1], total[1:2]

    kt, us = over_ctx(sums1, (one_s, one_r), kt, us)
    scale = 1.0 / math.sqrt(gene_count * ctx_n * dp_n)

    def query_pass(start, count, carry):
        at = pl.ds(start, count)
        u = unit[at, :width]
        qf = jnp.exp(feature_scale * u)
        den = head_sum(qf * kt, ones)
        att = head_sum(qf * us, ones) / den
        predicted = base_dot[at, 0:1] + jnp.sum(att, axis=1, keepdims=True) * (1.0 / HEAD)
        pred_x[at, :] = jnp.broadcast_to(predicted, (count, 128))
        res = (predicted - target_x[at, 0:1]) * (scale * keep_x[at, 0:1])
        qs = qf * (res / den)
        h = qs * (us - att * kt)
        back = head_sum(h * u, ones) * (1.0 / HEAD)
        rows[at, :width] = (feature_scale * inverse[at, :width] * (h - u * back)).astype(BF16)
        return (
            carry[0] + jnp.sum(qs, axis=0, keepdims=True),
            carry[1] - jnp.sum(qs * att, axis=0, keepdims=True),
        )

    cs, ts = lax.fori_loop(
        0,
        padded // chunk,
        lambda i, carry: query_pass(pl.multiple_of(i * chunk, 16), chunk, carry),
        (none, none),
    )
    cs, ts = query_pass(padded, tok_n, (cs, ts))
    cs, ts = over_ctx(sums2, (two_s, two_r), cs, ts)
    pick6 = jnp.where(
        lax.broadcasted_iota(jnp.int32, (width, 128), 0) // HEAD
        == lax.broadcasted_iota(jnp.int32, (width, 128), 1),
        1.0,
        0.0,
    ).astype(BF16)

    def key_pass(start, count):
        at = pl.ds(start, count)
        u = unit[at, width:]
        kf = jnp.exp(feature_scale * u) * keep_x[at, 0:1]
        h = kf * (vwx[at, :] * cs + ts)
        back = head_sum(h * u, ones) * (1.0 / HEAD)
        rows[at, width : 2 * width] = (
            feature_scale * inverse[at, width:] * (h - u * back)
        ).astype(BF16)
        high, low = split(kf * cs)
        kc_high, kc_low = split(mm(high, pick6) + mm(low, pick6))
        rows[at, 2 * width : 2 * width + 128] = kc_high
        rows[at, 2 * width + 128 :] = kc_low

    def key_step(i, carry):
        key_pass(pl.multiple_of(i * chunk, 16), chunk)
        return carry

    lax.fori_loop(0, padded // chunk, key_step, 0)
    key_pass(padded, tok_n)

    hit = gene_lane == idx_col
    tok_pred = pred_x[padded:, 0:1]
    base_row = jnp.transpose(pred_x[0:padded, :])[0:1, :]
    moved = jnp.sum(jnp.where(hit, tok_pred, 0.0), axis=0, keepdims=True)
    final = jnp.where(keep_row > 0.5, base_row, moved)
    pred_ref[...] = final[:, :gene_count]

    share = width // dp_n
    cols = grads.shape[2]
    full = lax.dot_general(
        normed[...], rows[...], (((0,), (0,)), ((), ())), preferred_element_type=F32
    )
    full = jnp.concatenate(
        [full[:, : 2 * width], full[:, 2 * width : cols] + full[:, cols:]], axis=1
    )
    for j in range(dp_n):
        grads[j] = full[j * share : (j + 1) * share, :]
    core = lax.rem(dp, 2)
    chip = dp // 2
    chips = dp_n // 2
    copies = []
    for z in range(chips):
        copies.append(
            send(
                grads.at[2 * z + 1 - core],
                core_recv.at[z],
                (core_s, core_r),
                z,
                z,
                {"dp": 2 * chip + 1 - core},
            )
        )
    for copy in copies:
        copy.wait()
    copies = []
    for k in range(1, chips):
        z = lax.rem(chip + k, chips)
        z_send[k] = (grads[2 * z + core] + core_recv[z]).astype(BF16)
        copies.append(
            send(z_send.at[k], z_recv.at[k], (z_s, z_r), k, k, {"dp": 2 * z + core})
        )
    total = grads[2 * chip + core] + core_recv[chip]
    for copy in copies:
        copy.wait()
    for k in range(1, chips):
        total = total + z_recv[k].astype(F32)
    span = ctx_recv.shape[2]
    for s in range(ctx_n):
        lo = 256 * min(s, 2)
        part[s] = total[:, lo : lo + span]
    copies = []
    for k in range(1, ctx_n):
        dest = lax.rem(ctx + k, ctx_n)
        copies.append(
            send(part.at[dest], ctx_recv.at[k], (last_s, last_r), k, k, {"ctx": dest})
        )
    for copy in copies:
        copy.wait()
    window = part[ctx]
    for k in range(1, ctx_n):
        window = window + ctx_recv[k]
    tail_part = window[:, 256:]
    head_of = lax.broadcasted_iota(jnp.int32, (1, width), 1) // HEAD
    value_grad = jnp.zeros((share, width), F32)
    for h in range(HEADS):
        value_grad = value_grad + tail_part[:, h : h + 1] * jnp.where(head_of == h, w_row, 0.0)
    result = window[:, 0:288]
    result = jnp.where(ctx == 1, window[:, 32:320], result)
    mixed = jnp.concatenate([window[:, 64:256], value_grad[:, 0:96]], axis=1)
    result = jnp.where(ctx == 2, mixed, result)
    result = jnp.where(ctx == 3, value_grad[:, 96:384], result)
    grad_ref[...] = result


def fused(
    gene_ids,
    counts,
    values,
    lengths,
    bin_edges,
    bin_table,
    value_weight,
    in_weight,
    out_weight,
    gene_table,
    zero_embed,
    qkv_weight,
    proj_weight,
    readout,
    targets,
):
    ctx_n = lax.axis_size("ctx")
    dp_n = lax.axis_size("dp")
    gene_count, width = gene_table.shape
    padded = -(-gene_count // 128) * 128
    tok_n = gene_ids.shape[1]
    chunk = padded // CHUNKS
    total = padded + tok_n
    share = width // dp_n
    gene_table = jnp.pad(gene_table, ((0, padded - gene_count), (0, 0)))
    targets = jnp.pad(targets, ((0, 0), (0, padded - gene_count)))
    vmem = pl.BlockSpec(memory_space=pltpu.VMEM)
    smem = pl.BlockSpec(memory_space=pltpu.SMEM)
    dma = pltpu.SemaphoreType.DMA
    cols = 2 * width + 128
    return pl.pallas_call(
        functools.partial(kernel, gene_count, chunk),
        out_shape=(
            jax.ShapeDtypeStruct((1, gene_count), F32),
            jax.ShapeDtypeStruct((share, 3 * width // ctx_n), F32),
        ),
        in_specs=[vmem] * 3 + [smem] * 2 + [vmem] * 10,
        out_specs=(vmem, vmem),
        scratch_shapes=[
            pltpu.VMEM((64, width), F32),
            pltpu.VMEM((256, 256), BF16),
            pltpu.VMEM((width, width), BF16),
            pltpu.VMEM((width, width), BF16),
            pltpu.VMEM((ctx_n, 8, tok_n), F32),
            pltpu.VMEM((dp_n, 8, tok_n), F32),
            pltpu.VMEM((dp_n, tok_n, width), BF16),
            pltpu.VMEM((dp_n, tok_n, width), BF16),
            pltpu.VMEM((total, width), BF16),
            pltpu.VMEM((total, 2 * width), F32),
            pltpu.VMEM((total, 2 * width), F32),
            pltpu.VMEM((total, width), F32),
            pltpu.VMEM((total, 2 * width + 256), BF16),
            pltpu.VMEM((total, 128), F32),
            pltpu.VMEM((total, 128), F32),
            pltpu.VMEM((total, 128), F32),
            pltpu.VMEM((total, 128), F32),
            pltpu.VMEM((ctx_n, 8, width), F32),
            pltpu.VMEM((ctx_n, 8, width), F32),
            pltpu.VMEM((dp_n, share, cols), F32),
            pltpu.VMEM((dp_n // 2, share, cols), F32),
            pltpu.VMEM((dp_n // 2, share, cols), BF16),
            pltpu.VMEM((dp_n // 2, share, cols), BF16),
            pltpu.VMEM((ctx_n, share, 384), F32),
            pltpu.VMEM((ctx_n, share, 384), F32),
        ]
        + [dma((n,)) for n in (ctx_n, dp_n, dp_n, ctx_n, ctx_n, dp_n // 2, dp_n // 2, ctx_n) for _ in range(2)],
        compiler_params=pltpu.CompilerParams(
            collective_id=0, has_side_effects=True, vmem_limit_bytes=60 * 2**20
        ),
        cost_estimate=pl.CostEstimate(
            flops=20 * total * width * width, bytes_accessed=6 * 2**20, transcendentals=4 * total * width
        ),
    )(
        gene_ids,
        counts,
        values,
        lengths,
        bin_edges,
        bin_table,
        value_weight[None, :],
        in_weight,
        out_weight,
        gene_table,
        zero_embed[None, :],
        qkv_weight,
        proj_weight,
        readout[None, :],
        targets,
    )


def program(*args):
    ctx_n = lax.axis_size("ctx")
    dp_n = lax.axis_size("dp")
    width = args[9].shape[1]
    fits = ctx_n == 4 and dp_n == 8 and width == 384 and args[0].shape[1] == 128
    fits = fits and args[9].shape[0] <= 2432
    return (fused if fits else body)(*args)


def solution(mesh):
    return jax.shard_map(
        program,
        mesh=mesh,
        in_specs=(
            P("dp", "ctx"),
            P("dp", "ctx"),
            P("dp", "ctx"),
            P("dp"),
            P("dp", None),
            P(),
            P(),
            P(None, "dp"),
            P("dp", None),
            P("ctx", None),
            P(),
            P(),
            P(),
            P(),
            P("dp", "ctx"),
        ),
        out_specs=(P("dp", "ctx"), P("dp", "ctx")),
        check_vma=False,
    )
```

```python
import functools
import math

import jax
import jax.numpy as jnp
from jax import lax
from jax.experimental import pallas as pl
from jax.experimental.pallas import tpu as pltpu
from jax.sharding import PartitionSpec as P

HEAD = 64
HEADS = 6
CHUNKS = 8


feature_scale = 2.5
norm_eps = 1e-06
highest = lax.Precision.HIGHEST


def featurize(projected):
    inverse = lax.rsqrt(jnp.mean(projected * projected, axis=-1, keepdims=True) + norm_eps)
    return jnp.exp(feature_scale * projected * inverse)


def rms_round(matrix):
    inverse = lax.rsqrt(jnp.mean(matrix * matrix, axis=-1, keepdims=True) + norm_eps)
    return (matrix * inverse).astype(jnp.bfloat16)


def embed_tokens(token_counts, token_values, cell_edges, bin_table, value_weight):
    binned = jnp.sum((token_counts[:, None] >= cell_edges[None, :]).astype(jnp.int32), axis=1)
    one_hot = (binned[:, None] == jnp.arange(bin_table.shape[0], dtype=jnp.int32)[None, :]).astype(
        jnp.bfloat16
    )
    looked = jnp.dot(one_hot, bin_table, preferred_element_type=jnp.float32)
    return looked + token_values[:, None] * value_weight[None, :]


def encode(token_counts, token_values, cell_edges, bin_table, value_weight, in_weight, out_weight):
    embedded = embed_tokens(token_counts, token_values, cell_edges, bin_table, value_weight)
    normed_tokens = rms_round(embedded)
    activated = jax.nn.silu(
        jnp.dot(
            normed_tokens,
            lax.all_gather(in_weight, "dp", axis=1, tiled=True),
            preferred_element_type=jnp.float32,
        )
    ).astype(jnp.bfloat16)
    mixed = embedded + jnp.dot(
        activated,
        lax.all_gather(out_weight, "dp", axis=0, tiled=True),
        preferred_element_type=jnp.float32,
    )
    return mixed.astype(jnp.bfloat16)


def assemble(gene_rows, local_index, arrived, zero_embed):
    row_count = gene_rows.shape[0]
    placed = (
        jnp.zeros((row_count, gene_rows.shape[1]), jnp.float32)
        .at[local_index]
        .set(arrived.astype(jnp.float32), mode="drop")
    )
    marked = jnp.zeros((row_count,), jnp.int32).at[local_index].set(1, mode="drop")
    filled = jnp.where(marked[:, None] == 1, placed, zero_embed.astype(jnp.float32)[None, :])
    return (gene_rows.astype(jnp.float32) + filled).astype(jnp.bfloat16)


def project_heads(normed, qkv_weight):
    projected = jnp.dot(normed, qkv_weight, preferred_element_type=jnp.float32)
    row_count = projected.shape[0]
    model_width = qkv_weight.shape[0]
    query_raw = projected[:, :model_width].reshape(row_count, HEADS, HEAD)
    key_raw = projected[:, model_width : 2 * model_width].reshape(row_count, HEADS, HEAD)
    value_raw = projected[:, 2 * model_width :].reshape(row_count, HEADS, HEAD)
    return (query_raw, key_raw, value_raw)


def summarize(key_feat, value_raw):
    summary = jnp.einsum("ghj,ghe->hje", key_feat, value_raw, precision=highest)
    return (summary, jnp.sum(key_feat, axis=0))


def attend(query_feat, summary, key_total):
    numerator = jnp.einsum("ghj,hje->ghe", query_feat, summary, precision=highest)
    denominator = jnp.einsum("ghj,hj->gh", query_feat, key_total, precision=highest)
    return (numerator / denominator[..., None], denominator)


def readout_pass(gene_input, attention, proj_weight, readout):
    attended = attention.reshape(attention.shape[0], -1).astype(jnp.bfloat16)
    hidden_out = gene_input.astype(jnp.float32) + jnp.dot(
        attended, proj_weight, preferred_element_type=jnp.float32
    )
    return jnp.sum(hidden_out * readout[None, :], axis=1)


def back_to_attention(residual_grad, readout, proj_weight):
    hidden_grad = (residual_grad[:, None] * readout[None, :]).astype(jnp.bfloat16)
    grad_attn = lax.dot_general(
        hidden_grad, proj_weight, (((1,), (1,)), ((), ())), preferred_element_type=jnp.float32
    )
    return grad_attn.reshape(grad_attn.shape[0], HEADS, HEAD)


def attention_grads(grad_attn, attention, denominator, summary, key_total, query_feat):
    grad_numer = grad_attn / denominator[..., None]
    grad_denom = -jnp.sum(grad_attn * attention, axis=-1) / denominator
    grad_qfeat = (
        jnp.einsum("ghe,hje->ghj", grad_numer, summary, precision=highest)
        + grad_denom[..., None] * key_total[None]
    )
    part_summary = jnp.einsum("ghj,ghe->hje", query_feat, grad_numer, precision=highest)
    part_total = jnp.einsum("ghj,gh->hj", query_feat, grad_denom, precision=highest)
    return (grad_qfeat, part_summary, part_total)


def key_value_grads(grad_summary, grad_total, key_feat, value_raw):
    grad_kfeat = (
        jnp.einsum("ghe,hje->ghj", value_raw, grad_summary, precision=highest) + grad_total[None]
    )
    grad_value = jnp.einsum("ghj,hje->ghe", key_feat, grad_summary, precision=highest)
    return (grad_kfeat, grad_value)


def input_grads(query_raw, key_raw, grad_qfeat, grad_kfeat, grad_value):
    row_count = query_raw.shape[0]
    grad_query = jax.vjp(featurize, query_raw)[1](grad_qfeat)[0]
    grad_key = jax.vjp(featurize, key_raw)[1](grad_kfeat)[0]
    joined = jnp.concatenate(
        [
            grad_query.reshape(row_count, -1),
            grad_key.reshape(row_count, -1),
            grad_value.reshape(row_count, -1),
        ],
        axis=1,
    )
    return joined.astype(jnp.bfloat16)


def body(
    gene_ids,
    counts,
    values,
    lengths,
    bin_edges,
    bin_table,
    value_weight,
    in_weight,
    out_weight,
    gene_table,
    zero_embed,
    qkv_weight,
    proj_weight,
    readout,
    targets,
):
    ctx_count = lax.axis_size("ctx")
    slot_count = gene_ids.shape[1]
    gene_count = gene_table.shape[0]
    capacity = slot_count // ctx_count
    position = lax.axis_index("ctx") * slot_count + jnp.arange(slot_count, dtype=jnp.int32)
    live_slot = position < lengths[0]
    gene_row = gene_ids[0]
    target_range = gene_row // gene_count
    sort_order = jnp.argsort(target_range, stable=True)
    local_offset = jnp.where(live_slot, gene_row - target_range * gene_count, gene_count)[
        sort_order
    ]
    cell_edges = bin_edges[0]
    packed = jnp.stack([counts[0][sort_order], local_offset], axis=0).reshape(
        2, ctx_count, capacity
    )
    moved_values, moved_ints = (
        lax.all_to_all(
            values[0][sort_order].reshape(1, ctx_count, capacity),
            "ctx",
            split_axis=1,
            concat_axis=1,
            tiled=True,
        ),
        lax.all_to_all(packed, "ctx", split_axis=1, concat_axis=1, tiled=True),
    )
    arrived_index = moved_ints[1].reshape(slot_count)
    arrived = encode(
        moved_ints[0].reshape(slot_count),
        moved_values.reshape(slot_count),
        cell_edges,
        bin_table,
        value_weight,
        in_weight,
        out_weight,
    )
    gene_input = assemble(gene_table, arrived_index, arrived, zero_embed)
    normed = rms_round(gene_input.astype(jnp.float32))
    query_raw, key_raw, value_raw = project_heads(normed, qkv_weight)
    query_feat = featurize(query_raw)
    key_feat = featurize(key_raw)
    part_summary, part_total = summarize(key_feat, value_raw)
    summary, key_total = lax.psum((part_summary, part_total), "ctx")
    attention, denominator = attend(query_feat, summary, key_total)
    predicted = readout_pass(gene_input, attention, proj_weight, readout)
    grad_scale = 1.0 / math.sqrt(gene_count * ctx_count * lax.axis_size("dp"))
    residual_grad = (predicted - targets[0]) * grad_scale
    grad_attn = back_to_attention(residual_grad, readout, proj_weight)
    grad_qfeat, part_gsummary, part_gtotal = attention_grads(
        grad_attn, attention, denominator, summary, key_total, query_feat
    )
    grad_summary, grad_total = lax.psum((part_gsummary, part_gtotal), "ctx")
    grad_kfeat, grad_value = key_value_grads(grad_summary, grad_total, key_feat, value_raw)
    grad_rows = input_grads(query_raw, key_raw, grad_qfeat, grad_kfeat, grad_value)
    row_share = lax.psum_scatter(
        lax.dot_general(
            normed, grad_rows, (((0,), (0,)), ((), ())), preferred_element_type=jnp.float32
        ),
        "dp",
        scatter_dimension=0,
        tiled=True,
    )
    grad_qkv = lax.psum_scatter(row_share, "ctx", scatter_dimension=1, tiled=True)
    return (predicted[None, :], grad_qkv)


MESH = pl.DeviceIdType.MESH
F32 = jnp.float32
BF16 = jnp.bfloat16


def mm(left, right):
    return jnp.dot(left, right, preferred_element_type=F32)


def split(x):
    high = x.astype(BF16)
    return high, (x - high.astype(F32)).astype(BF16)


def head_sum(x, ones, exact=False):
    pieces = split(x) if exact else (x.astype(BF16),)
    parts = []
    for start in range(0, x.shape[1], 256):
        width = min(256, x.shape[1] - start)
        block = ones[:width, :width]
        parts.append(sum(mm(piece[:, start : start + width], block) for piece in pieces))
    return jnp.concatenate(parts, axis=1)


def rms(x):
    return x * lax.rsqrt(jnp.mean(x * x, axis=-1, keepdims=True) + norm_eps)


def lanes_to_rows(row, rows=128):
    return jnp.transpose(jnp.broadcast_to(row, (rows, row.shape[1])))


def send(src, dst, sems, index_send, index_recv, device):
    copy = pltpu.make_async_remote_copy(
        src_ref=src,
        dst_ref=dst,
        send_sem=sems[0].at[index_send],
        recv_sem=sems[1].at[index_recv],
        device_id=device,
        device_id_type=MESH,
    )
    copy.start()
    return copy


def kernel(
    gene_count,
    chunk,
    ids_ref,
    counts_ref,
    values_ref,
    lengths_ref,
    edges_ref,
    table_ref,
    vweight_ref,
    in_ref,
    out_ref,
    gene_ref,
    zero_ref,
    qkv_ref,
    proj_ref,
    readout_ref,
    targets_ref,
    pred_ref,
    grad_ref,
    table,
    ones,
    wvw_hi,
    genes,
    target_row,
    slots,
    tokens,
    ff_pair,
    ff_core,
    ff_send,
    ff_recv,
    normed,
    unit,
    inverse,
    vwx,
    rows,
    base_dot,
    target_x,
    keep_x,
    pred_x,
    sums1,
    sums2,
    grads_q,
    core_q,
    zs_q,
    zr_q,
    grads_k,
    core_k,
    zs_k,
    zr_k,
    part,
    ctx_recv,
    slot_s,
    slot_r,
    tok_s,
    tok_r,
    pair_s,
    pair_r,
    ff_s,
    ff_r,
    one_s,
    one_r,
    two_s,
    two_r,
    cq_s,
    cq_r,
    zq_s,
    zq_r,
    ck_s,
    ck_r,
    zk_s,
    zk_r,
    last_s,
    last_r,
):
    ctx = lax.axis_index("ctx")
    dp = lax.axis_index("dp")
    ctx_n = slots.shape[0]
    dp_n = tokens.shape[0]
    padded = genes.shape[0]
    width = gene_ref.shape[1]
    tok_n = ids_ref.shape[1]
    cap = tok_n // ctx_n
    core = lax.rem(dp, 2)
    chip = dp // 2
    chips = dp_n // 2
    vweight = vweight_ref[...].reshape(1, width)
    zero = zero_ref[...].astype(F32).reshape(1, width)
    readout = readout_ref[...].reshape(1, width)

    barrier = pltpu.get_barrier_semaphore()
    for k in range(1, ctx_n):
        pl.semaphore_signal(
            barrier, inc=1, device_id={"ctx": lax.rem(ctx + k, ctx_n)}, device_id_type=MESH
        )
    for k in range(1, dp_n):
        pl.semaphore_signal(
            barrier, inc=1, device_id={"dp": lax.rem(dp + k, dp_n)}, device_id_type=MESH
        )

    counts = counts_ref[...]
    binned = jnp.zeros(counts.shape, F32)
    for j in range(edges_ref.shape[1]):
        binned = binned + jnp.where(counts >= edges_ref[0, j], 1.0, 0.0)
    lane = lax.broadcasted_iota(jnp.int32, (1, tok_n), 1)
    live = (ctx * tok_n + lane) < lengths_ref[0]
    gene_f = jnp.where(live, ids_ref[...].astype(F32), -1.0)
    sub = lax.broadcasted_iota(jnp.int32, (8, tok_n), 0)
    slots[ctx] = jnp.where(
        sub == 0, gene_f, jnp.where(sub == 1, binned, jnp.where(sub == 2, values_ref[...], 0.0))
    )
    pl.semaphore_wait(barrier, ctx_n + dp_n - 2)
    copies = []
    for k in range(1, ctx_n):
        copies.append(
            send(
                slots.at[ctx],
                slots.at[ctx],
                (slot_s, slot_r),
                k,
                k,
                {"ctx": lax.rem(ctx + k, ctx_n)},
            )
        )

    hrow = lax.broadcasted_iota(jnp.int32, (256, 256), 0) // HEAD
    hcol = lax.broadcasted_iota(jnp.int32, (256, 256), 1) // HEAD
    ones[...] = jnp.where(hrow == hcol, 1.0, 0.0).astype(BF16)
    w_col = jnp.sum(proj_ref[...].astype(F32) * readout, axis=1, keepdims=True)
    w_row = jnp.transpose(jnp.broadcast_to(w_col, (width, 128)))[0:1, :]
    v_dot = head_sum(qkv_ref[:, 2 * width :].astype(F32) * w_row, ones, True)
    wvw_hi[...] = v_dot.astype(BF16)
    table[...] = jnp.zeros_like(table)
    table[0 : table_ref.shape[0], :] = table_ref[...].astype(F32)
    table_b = table[...].astype(BF16)
    target_row[...] = jnp.zeros_like(target_row)
    target_row[:, 0:gene_count] = targets_ref[...]
    target_x[0:padded, :] = lanes_to_rows(target_row[...])
    genes[0:gene_count, :] = gene_ref[...].astype(F32)
    genes[gene_count:, :] = jnp.zeros((padded - gene_count, width), F32)
    for copy in copies:
        copy.wait()

    first = (ctx * gene_count).astype(F32)
    upper = jnp.where(
        lax.broadcasted_iota(jnp.int32, (tok_n, tok_n), 0)
        < lax.broadcasted_iota(jnp.int32, (tok_n, tok_n), 1),
        1.0,
        0.0,
    ).astype(BF16)
    place = lax.broadcasted_iota(jnp.int32, (cap, tok_n), 0).astype(F32)
    idx_parts, bin_parts, val_parts = [], [], []
    for s in range(ctx_n):
        held = slots[s]
        local = held - first
        inside = (held >= first) & (local < gene_count)
        inside = jnp.where(inside, 1.0, 0.0)
        rank = mm(inside.astype(BF16), upper)
        chosen = (inside[0:1] > 0.5) & (rank[0:1] == place)
        idx_parts.append(jnp.sum(jnp.where(chosen, local[0:1] + 1.0, 0.0), axis=1, keepdims=True))
        bin_parts.append(jnp.sum(jnp.where(chosen, held[1:2], 0.0), axis=1, keepdims=True))
        val_parts.append(jnp.sum(jnp.where(chosen, held[2:3], 0.0), axis=1, keepdims=True))
    idx_col = jnp.concatenate(idx_parts, axis=0) - 1.0
    bin_col = jnp.concatenate(bin_parts, axis=0)
    val_col = jnp.concatenate(val_parts, axis=0)
    square = lax.broadcasted_iota(jnp.int32, (tok_n, 128), 1)
    mine = jnp.transpose(
        jnp.where(square == 0, bin_col, jnp.where(square == 1, val_col, jnp.where(square == 2, idx_col, 0.0)))
    )
    tokens[dp] = mine[0:8]
    copies = []
    for k in range(1, dp_n):
        copies.append(
            send(
                tokens.at[dp], tokens.at[dp], (tok_s, tok_r), k, k, {"dp": lax.rem(dp + k, dp_n)}
            )
        )
    idx_row = mine[2:3]

    gene_lane = lax.broadcasted_iota(jnp.int32, (tok_n, padded), 1).astype(F32)
    hit = gene_lane == idx_col
    token_base = mm(jnp.where(hit, 1.0, 0.0).astype(BF16), genes[...].astype(BF16))
    taken = jnp.sum(jnp.where(hit, 1.0, 0.0), axis=0, keepdims=True)
    tok_target = jnp.sum(jnp.where(hit, target_row[...], 0.0), axis=1, keepdims=True)
    in_range = lax.broadcasted_iota(jnp.int32, (1, padded), 1) < gene_count
    keep_row = jnp.where(in_range & (taken < 0.5), 1.0, 0.0)
    keep_x[0:padded, :] = lanes_to_rows(keep_row)
    tok_live = jnp.where(idx_col > -0.5, 1.0, 0.0)
    keep_x[padded:, :] = jnp.broadcast_to(tok_live, (tok_n, 128))
    target_x[padded:, :] = jnp.broadcast_to(tok_target, (tok_n, 128))

    pick = lax.broadcasted_iota(jnp.int32, (1, table.shape[0]), 1).astype(F32)

    def embed(bin_c, val_c):
        one_hot = jnp.where(bin_c == pick, 1.0, 0.0).astype(BF16)
        return mm(one_hot, table_b) + val_c * vweight

    def feed(emb):
        pre = mm(rms(emb).astype(BF16), in_ref[...])
        act = (pre / (1.0 + jnp.exp(-pre))).astype(BF16)
        return mm(act, out_ref[...])

    for copy in copies:
        copy.wait()

    def unpack(cells):
        got = jnp.concatenate(
            [jnp.transpose(jnp.concatenate([tokens[c]] * (128 // 8), axis=0)) for c in cells], axis=0
        )
        return embed(got[:, 0:1], got[:, 1:2])

    half = feed(unpack([2 * z + 1 - core for z in range(chips)]))
    pair_copies = []
    for z in range(chips):
        ff_pair[z] = half[z * tok_n : (z + 1) * tok_n].astype(BF16)
        pair_copies.append(
            send(
                ff_pair.at[z], ff_core.at[z], (pair_s, pair_r), z, z, {"dp": 2 * chip + 1 - core}
            )
        )
    turn = [lax.rem(chip + k, chips) for k in range(chips)]
    own_emb = unpack([2 * z + core for z in turn])
    half = feed(own_emb)
    for copy in pair_copies:
        copy.wait()
    ff_copies = []
    for k in range(1, chips):
        mixed = half[k * tok_n : (k + 1) * tok_n] + ff_core[turn[k]].astype(F32)
        ff_send[k] = mixed.astype(BF16)
        ff_copies.append(
            send(ff_send.at[k], ff_recv.at[k], (ff_s, ff_r), k, k, {"dp": 2 * turn[k] + core})
        )
    own_mix = own_emb[0:tok_n] + half[0:tok_n] + ff_core[chip].astype(F32)

    def features(start, count, gene_input):
        at = pl.ds(start, count)
        gi = gene_input.astype(BF16).astype(F32)
        nb = rms(gi).astype(BF16)
        normed[at, :] = nb
        base_dot[at, :] = jnp.broadcast_to(
            jnp.sum(gi * readout, axis=1, keepdims=True), (count, 128)
        )
        raw = mm(nb, qkv_ref[:, : 2 * width])
        inv = lax.rsqrt(head_sum(raw * raw, ones, True) * (1.0 / HEAD) + norm_eps)
        u = raw * inv
        unit[at, :] = u
        inverse[at, :] = inv
        vw = mm(nb, wvw_hi[...])
        vwx[at, :] = vw
        kf = jnp.exp(feature_scale * u[:, width:]) * keep_x[at, 0:1]
        return (
            jnp.sum(kf, axis=0, keepdims=True),
            jnp.sum(kf * vw, axis=0, keepdims=True),
        )

    none = jnp.zeros((1, width), F32)

    def first_pass(i, carry):
        start = pl.multiple_of(i * chunk, 16)
        a, b = features(start, chunk, genes[pl.ds(start, chunk), :] + zero)
        return carry[0] + a, carry[1] + b

    kt, us = lax.fori_loop(0, padded // chunk, first_pass, (none, none))
    for copy in ff_copies:
        copy.wait()
    for k in range(1, chips):
        own_mix = own_mix + ff_recv[k].astype(F32)
    a, b = features(padded, tok_n, token_base + own_mix.astype(BF16).astype(F32))
    kt, us = kt + a, us + b

    def ctx_start(buffer, sems, x, y):
        row_at = lax.broadcasted_iota(jnp.int32, (8, width), 0)
        buffer[ctx] = jnp.where(row_at == 0, x, jnp.where(row_at == 1, y, 0.0))
        sent = []
        for k in range(1, ctx_n):
            sent.append(
                send(buffer.at[ctx], buffer.at[ctx], sems, k, k, {"ctx": lax.rem(ctx + k, ctx_n)})
            )
        return sent

    def ctx_finish(buffer, sent):
        for copy in sent:
            copy.wait()
        total = buffer[0]
        for s in range(1, ctx_n):
            total = total + buffer[s]
        return total[0:1], total[1:2]

    kt, us = ctx_finish(sums1, ctx_start(sums1, (one_s, one_r), kt, us))
    scale = 1.0 / math.sqrt(gene_count * ctx_n * dp_n)

    def query_pass(start, count, carry):
        at = pl.ds(start, count)
        u = unit[at, :width]
        qf = jnp.exp(feature_scale * u)
        den = head_sum(qf * kt, ones)
        att = head_sum(qf * us, ones) / den
        predicted = base_dot[at, 0:1] + jnp.sum(att, axis=1, keepdims=True) * (1.0 / HEAD)
        pred_x[at, :] = jnp.broadcast_to(predicted, (count, 128))
        res = (predicted - target_x[at, 0:1]) * (scale * keep_x[at, 0:1])
        qs = qf * (res / den)
        h = qs * (us - att * kt)
        back = head_sum(h * u, ones) * (1.0 / HEAD)
        rows[at, :width] = (feature_scale * inverse[at, :width] * (h - u * back)).astype(BF16)
        return (
            carry[0] + jnp.sum(qs, axis=0, keepdims=True),
            carry[1] - jnp.sum(qs * att, axis=0, keepdims=True),
        )

    cs, ts = lax.fori_loop(
        0,
        padded // chunk,
        lambda i, carry: query_pass(pl.multiple_of(i * chunk, 16), chunk, carry),
        (none, none),
    )
    cs, ts = query_pass(padded, tok_n, (cs, ts))
    sent = ctx_start(sums2, (two_s, two_r), cs, ts)

    share = width // dp_n

    def core_start(part_grad, grads, recv, sems):
        for j in range(dp_n):
            grads[j] = part_grad[j * share : (j + 1) * share, :]
        return [
            send(
                grads.at[2 * z + 1 - core], recv.at[z], sems, z, z, {"dp": 2 * chip + 1 - core}
            )
            for z in range(chips)
        ]

    def z_start(core_copies, grads, recv, out, into, sems):
        for copy in core_copies:
            copy.wait()
        started = []
        for k in range(1, chips):
            z = lax.rem(chip + k, chips)
            out[k] = (grads[2 * z + core] + recv[z]).astype(BF16)
            started.append(send(out.at[k], into.at[k], sems, k, k, {"dp": 2 * z + core}))
        return grads[2 * chip + core] + recv[chip], started

    def z_finish(total, started, into):
        for copy in started:
            copy.wait()
        for k in range(1, chips):
            total = total + into[k].astype(F32)
        return total

    def outer(lo, hi):
        return lax.dot_general(
            normed[...], rows[:, lo:hi], (((0,), (0,)), ((), ())), preferred_element_type=F32
        )

    copies_q = core_start(outer(0, width), grads_q, core_q, (cq_s, cq_r))
    cs, ts = ctx_finish(sums2, sent)
    pick6 = jnp.where(
        lax.broadcasted_iota(jnp.int32, (width, 128), 0) // HEAD
        == lax.broadcasted_iota(jnp.int32, (width, 128), 1),
        1.0,
        0.0,
    ).astype(BF16)

    def key_pass(start, count):
        at = pl.ds(start, count)
        u = unit[at, width:]
        kf = jnp.exp(feature_scale * u) * keep_x[at, 0:1]
        h = kf * (vwx[at, :] * cs + ts)
        back = head_sum(h * u, ones) * (1.0 / HEAD)
        rows[at, width : 2 * width] = (
            feature_scale * inverse[at, width:] * (h - u * back)
        ).astype(BF16)
        rows[at, 2 * width :] = mm((kf * cs).astype(BF16), pick6).astype(BF16)

    def key_step(i, carry):
        key_pass(pl.multiple_of(i * chunk, 16), chunk)
        return carry

    steps = padded // chunk
    lax.fori_loop(0, steps // 2, key_step, 0)
    total_q, started_q = z_start(copies_q, grads_q, core_q, zs_q, zr_q, (zq_s, zq_r))
    lax.fori_loop(steps // 2, steps, key_step, 0)
    key_pass(padded, tok_n)
    copies_k = core_start(outer(width, 2 * width + 128), grads_k, core_k, (ck_s, ck_r))
    total_k, started_k = z_start(copies_k, grads_k, core_k, zs_k, zr_k, (zk_s, zk_r))

    hit = gene_lane == idx_col
    tok_pred = pred_x[padded:, 0:1]
    base_row = jnp.transpose(pred_x[0:padded, :])[0:1, :]
    moved = jnp.sum(jnp.where(hit, tok_pred, 0.0), axis=0, keepdims=True)
    final = jnp.where(keep_row > 0.5, base_row, moved)
    pred_ref[...] = final[:, :gene_count]

    total = jnp.concatenate(
        [z_finish(total_q, started_q, zr_q), z_finish(total_k, started_k, zr_k)], axis=1
    )
    span = ctx_recv.shape[2]
    for s in range(ctx_n):
        lo = 256 * min(s, 2)
        part[s] = total[:, lo : lo + span]
    copies = []
    for k in range(1, ctx_n):
        dest = lax.rem(ctx + k, ctx_n)
        copies.append(
            send(part.at[dest], ctx_recv.at[k], (last_s, last_r), k, k, {"ctx": dest})
        )
    for copy in copies:
        copy.wait()
    window = part[ctx]
    for k in range(1, ctx_n):
        window = window + ctx_recv[k]
    tail_part = window[:, 256:]
    head_of = lax.broadcasted_iota(jnp.int32, (1, width), 1) // HEAD
    value_grad = jnp.zeros((share, width), F32)
    for h in range(HEADS):
        value_grad = value_grad + tail_part[:, h : h + 1] * jnp.where(head_of == h, w_row, 0.0)
    result = window[:, 0:288]
    result = jnp.where(ctx == 1, window[:, 32:320], result)
    mixed = jnp.concatenate([window[:, 64:256], value_grad[:, 0:96]], axis=1)
    result = jnp.where(ctx == 2, mixed, result)
    result = jnp.where(ctx == 3, value_grad[:, 96:384], result)
    grad_ref[...] = result


def fused(
    gene_ids,
    counts,
    values,
    lengths,
    bin_edges,
    bin_table,
    value_weight,
    in_weight,
    out_weight,
    gene_table,
    zero_embed,
    qkv_weight,
    proj_weight,
    readout,
    targets,
):
    ctx_n = lax.axis_size("ctx")
    dp_n = lax.axis_size("dp")
    gene_count, width = gene_table.shape
    padded = -(-gene_count // 128) * 128
    tok_n = gene_ids.shape[1]
    chunk = padded // CHUNKS
    total = padded + tok_n
    share = width // dp_n
    vmem = pl.BlockSpec(memory_space=pltpu.VMEM)
    smem = pl.BlockSpec(memory_space=pltpu.SMEM)
    dma = pltpu.SemaphoreType.DMA
    chips = dp_n // 2
    return pl.pallas_call(
        functools.partial(kernel, gene_count, chunk),
        out_shape=(
            jax.ShapeDtypeStruct((1, gene_count), F32),
            jax.ShapeDtypeStruct((share, 3 * width // ctx_n), F32),
        ),
        in_specs=[vmem] * 3 + [smem] * 2 + [vmem] * 10,
        out_specs=(vmem, vmem),
        scratch_shapes=[
            pltpu.VMEM((64, width), F32),
            pltpu.VMEM((256, 256), BF16),
            pltpu.VMEM((width, width), BF16),
            pltpu.VMEM((padded, width), F32),
            pltpu.VMEM((1, padded), F32),
            pltpu.VMEM((ctx_n, 8, tok_n), F32),
            pltpu.VMEM((dp_n, 8, tok_n), F32),
            pltpu.VMEM((chips, tok_n, width), BF16),
            pltpu.VMEM((chips, tok_n, width), BF16),
            pltpu.VMEM((chips, tok_n, width), BF16),
            pltpu.VMEM((chips, tok_n, width), BF16),
            pltpu.VMEM((total, width), BF16),
            pltpu.VMEM((total, 2 * width), F32),
            pltpu.VMEM((total, 2 * width), F32),
            pltpu.VMEM((total, width), F32),
            pltpu.VMEM((total, 2 * width + 128), BF16),
            pltpu.VMEM((total, 128), F32),
            pltpu.VMEM((total, 128), F32),
            pltpu.VMEM((total, 128), F32),
            pltpu.VMEM((total, 128), F32),
            pltpu.VMEM((ctx_n, 8, width), F32),
            pltpu.VMEM((ctx_n, 8, width), F32),
            pltpu.VMEM((dp_n, share, width), F32),
            pltpu.VMEM((chips, share, width), F32),
            pltpu.VMEM((chips, share, width), BF16),
            pltpu.VMEM((chips, share, width), BF16),
            pltpu.VMEM((dp_n, share, width + 128), F32),
            pltpu.VMEM((chips, share, width + 128), F32),
            pltpu.VMEM((chips, share, width + 128), BF16),
            pltpu.VMEM((chips, share, width + 128), BF16),
            pltpu.VMEM((ctx_n, share, 384), F32),
            pltpu.VMEM((ctx_n, share, 384), F32),
        ]
        + [dma((n,)) for n in (ctx_n, dp_n, chips, chips, ctx_n, ctx_n, chips, chips, chips, chips, ctx_n) for _ in range(2)],
        compiler_params=pltpu.CompilerParams(
            collective_id=0, has_side_effects=True, vmem_limit_bytes=60 * 2**20
        ),
        cost_estimate=pl.CostEstimate(
            flops=20 * total * width * width, bytes_accessed=6 * 2**20, transcendentals=4 * total * width
        ),
    )(
        gene_ids,
        counts,
        values,
        lengths,
        bin_edges,
        bin_table,
        value_weight,
        in_weight,
        out_weight,
        gene_table,
        zero_embed,
        qkv_weight,
        proj_weight,
        readout,
        targets,
    )


def program(*args):
    ctx_n = lax.axis_size("ctx")
    dp_n = lax.axis_size("dp")
    width = args[9].shape[1]
    fits = ctx_n == 4 and dp_n == 8 and width == 384 and args[0].shape[1] == 128
    fits = fits and args[9].shape[0] <= 2432
    return (fused if fits else body)(*args)


def solution(mesh):
    return jax.shard_map(
        program,
        mesh=mesh,
        in_specs=(
            P("dp", "ctx"),
            P("dp", "ctx"),
            P("dp", "ctx"),
            P("dp"),
            P("dp", None),
            P(),
            P(),
            P(None, "dp"),
            P("dp", None),
            P("ctx", None),
            P(),
            P(),
            P(),
            P(),
            P("dp", "ctx"),
        ),
        out_specs=(P("dp", "ctx"), P("dp", "ctx")),
        check_vma=False,
    )
```

```python
import functools
import math

import jax
import jax.numpy as jnp
from jax import lax
from jax.experimental import pallas as pl
from jax.experimental.pallas import tpu as pltpu
from jax.sharding import PartitionSpec as P

HEAD = 64
HEADS = 6
CHUNKS = 8


feature_scale = 2.5
norm_eps = 1e-06
highest = lax.Precision.HIGHEST


def featurize(projected):
    inverse = lax.rsqrt(jnp.mean(projected * projected, axis=-1, keepdims=True) + norm_eps)
    return jnp.exp(feature_scale * projected * inverse)


def rms_round(matrix):
    inverse = lax.rsqrt(jnp.mean(matrix * matrix, axis=-1, keepdims=True) + norm_eps)
    return (matrix * inverse).astype(jnp.bfloat16)


def embed_tokens(token_counts, token_values, cell_edges, bin_table, value_weight):
    binned = jnp.sum((token_counts[:, None] >= cell_edges[None, :]).astype(jnp.int32), axis=1)
    one_hot = (binned[:, None] == jnp.arange(bin_table.shape[0], dtype=jnp.int32)[None, :]).astype(
        jnp.bfloat16
    )
    looked = jnp.dot(one_hot, bin_table, preferred_element_type=jnp.float32)
    return looked + token_values[:, None] * value_weight[None, :]


def encode(token_counts, token_values, cell_edges, bin_table, value_weight, in_weight, out_weight):
    embedded = embed_tokens(token_counts, token_values, cell_edges, bin_table, value_weight)
    normed_tokens = rms_round(embedded)
    activated = jax.nn.silu(
        jnp.dot(
            normed_tokens,
            lax.all_gather(in_weight, "dp", axis=1, tiled=True),
            preferred_element_type=jnp.float32,
        )
    ).astype(jnp.bfloat16)
    mixed = embedded + jnp.dot(
        activated,
        lax.all_gather(out_weight, "dp", axis=0, tiled=True),
        preferred_element_type=jnp.float32,
    )
    return mixed.astype(jnp.bfloat16)


def assemble(gene_rows, local_index, arrived, zero_embed):
    row_count = gene_rows.shape[0]
    placed = (
        jnp.zeros((row_count, gene_rows.shape[1]), jnp.float32)
        .at[local_index]
        .set(arrived.astype(jnp.float32), mode="drop")
    )
    marked = jnp.zeros((row_count,), jnp.int32).at[local_index].set(1, mode="drop")
    filled = jnp.where(marked[:, None] == 1, placed, zero_embed.astype(jnp.float32)[None, :])
    return (gene_rows.astype(jnp.float32) + filled).astype(jnp.bfloat16)


def project_heads(normed, qkv_weight):
    projected = jnp.dot(normed, qkv_weight, preferred_element_type=jnp.float32)
    row_count = projected.shape[0]
    model_width = qkv_weight.shape[0]
    query_raw = projected[:, :model_width].reshape(row_count, HEADS, HEAD)
    key_raw = projected[:, model_width : 2 * model_width].reshape(row_count, HEADS, HEAD)
    value_raw = projected[:, 2 * model_width :].reshape(row_count, HEADS, HEAD)
    return (query_raw, key_raw, value_raw)


def summarize(key_feat, value_raw):
    summary = jnp.einsum("ghj,ghe->hje", key_feat, value_raw, precision=highest)
    return (summary, jnp.sum(key_feat, axis=0))


def attend(query_feat, summary, key_total):
    numerator = jnp.einsum("ghj,hje->ghe", query_feat, summary, precision=highest)
    denominator = jnp.einsum("ghj,hj->gh", query_feat, key_total, precision=highest)
    return (numerator / denominator[..., None], denominator)


def readout_pass(gene_input, attention, proj_weight, readout):
    attended = attention.reshape(attention.shape[0], -1).astype(jnp.bfloat16)
    hidden_out = gene_input.astype(jnp.float32) + jnp.dot(
        attended, proj_weight, preferred_element_type=jnp.float32
    )
    return jnp.sum(hidden_out * readout[None, :], axis=1)


def back_to_attention(residual_grad, readout, proj_weight):
    hidden_grad = (residual_grad[:, None] * readout[None, :]).astype(jnp.bfloat16)
    grad_attn = lax.dot_general(
        hidden_grad, proj_weight, (((1,), (1,)), ((), ())), preferred_element_type=jnp.float32
    )
    return grad_attn.reshape(grad_attn.shape[0], HEADS, HEAD)


def attention_grads(grad_attn, attention, denominator, summary, key_total, query_feat):
    grad_numer = grad_attn / denominator[..., None]
    grad_denom = -jnp.sum(grad_attn * attention, axis=-1) / denominator
    grad_qfeat = (
        jnp.einsum("ghe,hje->ghj", grad_numer, summary, precision=highest)
        + grad_denom[..., None] * key_total[None]
    )
    part_summary = jnp.einsum("ghj,ghe->hje", query_feat, grad_numer, precision=highest)
    part_total = jnp.einsum("ghj,gh->hj", query_feat, grad_denom, precision=highest)
    return (grad_qfeat, part_summary, part_total)


def key_value_grads(grad_summary, grad_total, key_feat, value_raw):
    grad_kfeat = (
        jnp.einsum("ghe,hje->ghj", value_raw, grad_summary, precision=highest) + grad_total[None]
    )
    grad_value = jnp.einsum("ghj,hje->ghe", key_feat, grad_summary, precision=highest)
    return (grad_kfeat, grad_value)


def input_grads(query_raw, key_raw, grad_qfeat, grad_kfeat, grad_value):
    row_count = query_raw.shape[0]
    grad_query = jax.vjp(featurize, query_raw)[1](grad_qfeat)[0]
    grad_key = jax.vjp(featurize, key_raw)[1](grad_kfeat)[0]
    joined = jnp.concatenate(
        [
            grad_query.reshape(row_count, -1),
            grad_key.reshape(row_count, -1),
            grad_value.reshape(row_count, -1),
        ],
        axis=1,
    )
    return joined.astype(jnp.bfloat16)


def body(
    gene_ids,
    counts,
    values,
    lengths,
    bin_edges,
    bin_table,
    value_weight,
    in_weight,
    out_weight,
    gene_table,
    zero_embed,
    qkv_weight,
    proj_weight,
    readout,
    targets,
):
    ctx_count = lax.axis_size("ctx")
    slot_count = gene_ids.shape[1]
    gene_count = gene_table.shape[0]
    capacity = slot_count // ctx_count
    position = lax.axis_index("ctx") * slot_count + jnp.arange(slot_count, dtype=jnp.int32)
    live_slot = position < lengths[0]
    gene_row = gene_ids[0]
    target_range = gene_row // gene_count
    sort_order = jnp.argsort(target_range, stable=True)
    local_offset = jnp.where(live_slot, gene_row - target_range * gene_count, gene_count)[
        sort_order
    ]
    cell_edges = bin_edges[0]
    packed = jnp.stack([counts[0][sort_order], local_offset], axis=0).reshape(
        2, ctx_count, capacity
    )
    moved_values, moved_ints = (
        lax.all_to_all(
            values[0][sort_order].reshape(1, ctx_count, capacity),
            "ctx",
            split_axis=1,
            concat_axis=1,
            tiled=True,
        ),
        lax.all_to_all(packed, "ctx", split_axis=1, concat_axis=1, tiled=True),
    )
    arrived_index = moved_ints[1].reshape(slot_count)
    arrived = encode(
        moved_ints[0].reshape(slot_count),
        moved_values.reshape(slot_count),
        cell_edges,
        bin_table,
        value_weight,
        in_weight,
        out_weight,
    )
    gene_input = assemble(gene_table, arrived_index, arrived, zero_embed)
    normed = rms_round(gene_input.astype(jnp.float32))
    query_raw, key_raw, value_raw = project_heads(normed, qkv_weight)
    query_feat = featurize(query_raw)
    key_feat = featurize(key_raw)
    part_summary, part_total = summarize(key_feat, value_raw)
    summary, key_total = lax.psum((part_summary, part_total), "ctx")
    attention, denominator = attend(query_feat, summary, key_total)
    predicted = readout_pass(gene_input, attention, proj_weight, readout)
    grad_scale = 1.0 / math.sqrt(gene_count * ctx_count * lax.axis_size("dp"))
    residual_grad = (predicted - targets[0]) * grad_scale
    grad_attn = back_to_attention(residual_grad, readout, proj_weight)
    grad_qfeat, part_gsummary, part_gtotal = attention_grads(
        grad_attn, attention, denominator, summary, key_total, query_feat
    )
    grad_summary, grad_total = lax.psum((part_gsummary, part_gtotal), "ctx")
    grad_kfeat, grad_value = key_value_grads(grad_summary, grad_total, key_feat, value_raw)
    grad_rows = input_grads(query_raw, key_raw, grad_qfeat, grad_kfeat, grad_value)
    row_share = lax.psum_scatter(
        lax.dot_general(
            normed, grad_rows, (((0,), (0,)), ((), ())), preferred_element_type=jnp.float32
        ),
        "dp",
        scatter_dimension=0,
        tiled=True,
    )
    grad_qkv = lax.psum_scatter(row_share, "ctx", scatter_dimension=1, tiled=True)
    return (predicted[None, :], grad_qkv)


MESH = pl.DeviceIdType.MESH
F32 = jnp.float32
BF16 = jnp.bfloat16


def mm(left, right):
    return jnp.dot(left, right, preferred_element_type=F32)


def split(x):
    high = x.astype(BF16)
    return high, (x - high.astype(F32)).astype(BF16)


def head_sum(x, ones, exact=False):
    pieces = split(x) if exact else (x.astype(BF16),)
    parts = []
    for start in range(0, x.shape[1], 256):
        width = min(256, x.shape[1] - start)
        block = ones[:width, :width]
        parts.append(sum(mm(piece[:, start : start + width], block) for piece in pieces))
    return jnp.concatenate(parts, axis=1)


def rms(x):
    return x * lax.rsqrt(jnp.mean(x * x, axis=-1, keepdims=True) + norm_eps)


def lanes_to_rows(row, rows=128):
    return jnp.transpose(jnp.broadcast_to(row, (rows, row.shape[1])))


def send(src, dst, sems, index_send, index_recv, device):
    copy = pltpu.make_async_remote_copy(
        src_ref=src,
        dst_ref=dst,
        send_sem=sems[0].at[index_send],
        recv_sem=sems[1].at[index_recv],
        device_id=device,
        device_id_type=MESH,
    )
    copy.start()
    return copy


def kernel(
    gene_count,
    chunk,
    ids_ref,
    counts_ref,
    values_ref,
    lengths_ref,
    edges_ref,
    table_ref,
    vweight_ref,
    in_ref,
    out_ref,
    gene_ref,
    zero_ref,
    qkv_ref,
    proj_ref,
    readout_ref,
    targets_ref,
    pred_ref,
    grad_ref,
    table,
    ones,
    wvw_hi,
    wvw_lo,
    genes,
    target_row,
    slots,
    tokens,
    ff_pair,
    ff_core,
    ff_send,
    ff_recv,
    normed,
    unit,
    inverse,
    vwx,
    rows,
    base_dot,
    target_x,
    keep_x,
    pred_x,
    sums1,
    sums2,
    grads_q,
    core_q,
    zs_q,
    zr_q,
    grads_k,
    core_k,
    zs_k,
    zr_k,
    part,
    ctx_recv,
    slot_s,
    slot_r,
    tok_s,
    tok_r,
    pair_s,
    pair_r,
    ff_s,
    ff_r,
    one_s,
    one_r,
    two_s,
    two_r,
    cq_s,
    cq_r,
    zq_s,
    zq_r,
    ck_s,
    ck_r,
    zk_s,
    zk_r,
    last_s,
    last_r,
):
    ctx = lax.axis_index("ctx")
    dp = lax.axis_index("dp")
    ctx_n = slots.shape[0]
    dp_n = tokens.shape[0]
    padded = genes.shape[0]
    width = gene_ref.shape[1]
    tok_n = ids_ref.shape[1]
    cap = tok_n // ctx_n
    core = lax.rem(dp, 2)
    chip = dp // 2
    chips = dp_n // 2
    vweight = vweight_ref[...].reshape(1, width)
    zero = zero_ref[...].astype(F32).reshape(1, width)
    readout = readout_ref[...].reshape(1, width)

    barrier = pltpu.get_barrier_semaphore()
    for k in range(1, ctx_n):
        pl.semaphore_signal(
            barrier, inc=1, device_id={"ctx": lax.rem(ctx + k, ctx_n)}, device_id_type=MESH
        )
    for k in range(1, dp_n):
        pl.semaphore_signal(
            barrier, inc=1, device_id={"dp": lax.rem(dp + k, dp_n)}, device_id_type=MESH
        )

    counts = counts_ref[...]
    binned = jnp.zeros(counts.shape, F32)
    for j in range(edges_ref.shape[1]):
        binned = binned + jnp.where(counts >= edges_ref[0, j], 1.0, 0.0)
    lane = lax.broadcasted_iota(jnp.int32, (1, tok_n), 1)
    live = (ctx * tok_n + lane) < lengths_ref[0]
    gene_f = jnp.where(live, ids_ref[...].astype(F32), -1.0)
    sub = lax.broadcasted_iota(jnp.int32, (8, tok_n), 0)
    slots[ctx] = jnp.where(
        sub == 0, gene_f, jnp.where(sub == 1, binned, jnp.where(sub == 2, values_ref[...], 0.0))
    )
    pl.semaphore_wait(barrier, ctx_n + dp_n - 2)
    copies = []
    for k in range(1, ctx_n):
        copies.append(
            send(
                slots.at[ctx],
                slots.at[ctx],
                (slot_s, slot_r),
                k,
                k,
                {"ctx": lax.rem(ctx + k, ctx_n)},
            )
        )

    hrow = lax.broadcasted_iota(jnp.int32, (256, 256), 0) // HEAD
    hcol = lax.broadcasted_iota(jnp.int32, (256, 256), 1) // HEAD
    ones[...] = jnp.where(hrow == hcol, 1.0, 0.0).astype(BF16)
    w_col = jnp.sum(proj_ref[...].astype(F32) * readout, axis=1, keepdims=True)
    w_row = jnp.transpose(jnp.broadcast_to(w_col, (width, 128)))[0:1, :]
    v_dot = head_sum(qkv_ref[:, 2 * width :].astype(F32) * w_row, ones, True)
    wvw_hi[...], wvw_lo[...] = split(v_dot)
    table[...] = jnp.zeros_like(table)
    table[0 : table_ref.shape[0], :] = table_ref[...].astype(F32)
    table_b = table[...].astype(BF16)
    target_row[...] = jnp.zeros_like(target_row)
    target_row[:, 0:gene_count] = targets_ref[...]
    target_x[0:padded, :] = lanes_to_rows(target_row[...])
    genes[0:gene_count, :] = gene_ref[...].astype(F32)
    genes[gene_count:, :] = jnp.zeros((padded - gene_count, width), F32)
    for copy in copies:
        copy.wait()

    first = (ctx * gene_count).astype(F32)
    upper = jnp.where(
        lax.broadcasted_iota(jnp.int32, (tok_n, tok_n), 0)
        < lax.broadcasted_iota(jnp.int32, (tok_n, tok_n), 1),
        1.0,
        0.0,
    ).astype(BF16)
    place = lax.broadcasted_iota(jnp.int32, (cap, tok_n), 0).astype(F32)
    idx_parts, bin_parts, val_parts = [], [], []
    for s in range(ctx_n):
        held = slots[s]
        local = held - first
        inside = (held >= first) & (local < gene_count)
        inside = jnp.where(inside, 1.0, 0.0)
        rank = mm(inside.astype(BF16), upper)
        chosen = (inside[0:1] > 0.5) & (rank[0:1] == place)
        idx_parts.append(jnp.sum(jnp.where(chosen, local[0:1] + 1.0, 0.0), axis=1, keepdims=True))
        bin_parts.append(jnp.sum(jnp.where(chosen, held[1:2], 0.0), axis=1, keepdims=True))
        val_parts.append(jnp.sum(jnp.where(chosen, held[2:3], 0.0), axis=1, keepdims=True))
    idx_col = jnp.concatenate(idx_parts, axis=0) - 1.0
    bin_col = jnp.concatenate(bin_parts, axis=0)
    val_col = jnp.concatenate(val_parts, axis=0)
    square = lax.broadcasted_iota(jnp.int32, (tok_n, 128), 1)
    mine = jnp.transpose(
        jnp.where(square == 0, bin_col, jnp.where(square == 1, val_col, jnp.where(square == 2, idx_col, 0.0)))
    )
    tokens[dp] = mine[0:8]
    copies = []
    for k in range(1, dp_n):
        copies.append(
            send(
                tokens.at[dp], tokens.at[dp], (tok_s, tok_r), k, k, {"dp": lax.rem(dp + k, dp_n)}
            )
        )
    idx_row = mine[2:3]

    gene_lane = lax.broadcasted_iota(jnp.int32, (tok_n, padded), 1).astype(F32)
    hit = gene_lane == idx_col
    token_base = mm(jnp.where(hit, 1.0, 0.0).astype(BF16), genes[...].astype(BF16))
    taken = jnp.sum(jnp.where(hit, 1.0, 0.0), axis=0, keepdims=True)
    tok_target = jnp.sum(jnp.where(hit, target_row[...], 0.0), axis=1, keepdims=True)
    in_range = lax.broadcasted_iota(jnp.int32, (1, padded), 1) < gene_count
    keep_row = jnp.where(in_range & (taken < 0.5), 1.0, 0.0)
    keep_x[0:padded, :] = lanes_to_rows(keep_row)
    tok_live = jnp.where(idx_col > -0.5, 1.0, 0.0)
    keep_x[padded:, :] = jnp.broadcast_to(tok_live, (tok_n, 128))
    target_x[padded:, :] = jnp.broadcast_to(tok_target, (tok_n, 128))

    pick = lax.broadcasted_iota(jnp.int32, (1, table.shape[0]), 1).astype(F32)

    def embed(bin_c, val_c):
        one_hot = jnp.where(bin_c == pick, 1.0, 0.0).astype(BF16)
        return mm(one_hot, table_b) + val_c * vweight

    def feed(emb):
        pre = mm(rms(emb).astype(BF16), in_ref[...])
        act = (pre / (1.0 + jnp.exp(-pre))).astype(BF16)
        return mm(act, out_ref[...])

    for copy in copies:
        copy.wait()

    def unpack(cells):
        got = jnp.concatenate(
            [jnp.transpose(jnp.concatenate([tokens[c]] * (128 // 8), axis=0)) for c in cells], axis=0
        )
        return embed(got[:, 0:1], got[:, 1:2])

    half = feed(unpack([2 * z + 1 - core for z in range(chips)]))
    pair_copies = []
    for z in range(chips):
        ff_pair[z] = half[z * tok_n : (z + 1) * tok_n].astype(BF16)
        pair_copies.append(
            send(
                ff_pair.at[z], ff_core.at[z], (pair_s, pair_r), z, z, {"dp": 2 * chip + 1 - core}
            )
        )
    turn = [lax.rem(chip + k, chips) for k in range(chips)]
    own_emb = unpack([2 * z + core for z in turn])
    half = feed(own_emb)
    for copy in pair_copies:
        copy.wait()
    ff_copies = []
    for k in range(1, chips):
        mixed = half[k * tok_n : (k + 1) * tok_n] + ff_core[turn[k]].astype(F32)
        ff_send[k] = mixed.astype(BF16)
        ff_copies.append(
            send(ff_send.at[k], ff_recv.at[k], (ff_s, ff_r), k, k, {"dp": 2 * turn[k] + core})
        )
    own_mix = own_emb[0:tok_n] + half[0:tok_n] + ff_core[chip].astype(F32)

    def features(start, count, gene_input):
        at = pl.ds(start, count)
        gi = gene_input.astype(BF16).astype(F32)
        nb = rms(gi).astype(BF16)
        normed[at, :] = nb
        base_dot[at, :] = jnp.broadcast_to(
            jnp.sum(gi * readout, axis=1, keepdims=True), (count, 128)
        )
        raw = mm(nb, qkv_ref[:, : 2 * width])
        inv = lax.rsqrt(head_sum(raw * raw, ones, True) * (1.0 / HEAD) + norm_eps)
        u = raw * inv
        unit[at, :] = u
        inverse[at, :] = inv
        vw = mm(nb, wvw_hi[...]) + mm(nb, wvw_lo[...])
        vwx[at, :] = vw
        kf = jnp.exp(feature_scale * u[:, width:]) * keep_x[at, 0:1]
        return (
            jnp.sum(kf, axis=0, keepdims=True),
            jnp.sum(kf * vw, axis=0, keepdims=True),
        )

    none = jnp.zeros((1, width), F32)

    def first_pass(i, carry):
        start = pl.multiple_of(i * chunk, 16)
        a, b = features(start, chunk, genes[pl.ds(start, chunk), :] + zero)
        return carry[0] + a, carry[1] + b

    kt, us = lax.fori_loop(0, padded // chunk, first_pass, (none, none))
    for copy in ff_copies:
        copy.wait()
    for k in range(1, chips):
        own_mix = own_mix + ff_recv[k].astype(F32)
    a, b = features(padded, tok_n, token_base + own_mix.astype(BF16).astype(F32))
    kt, us = kt + a, us + b

    def ctx_start(buffer, sems, x, y):
        row_at = lax.broadcasted_iota(jnp.int32, (8, width), 0)
        buffer[ctx] = jnp.where(row_at == 0, x, jnp.where(row_at == 1, y, 0.0))
        sent = []
        for k in range(1, ctx_n):
            sent.append(
                send(buffer.at[ctx], buffer.at[ctx], sems, k, k, {"ctx": lax.rem(ctx + k, ctx_n)})
            )
        return sent

    def ctx_finish(buffer, sent):
        for copy in sent:
            copy.wait()
        total = buffer[0]
        for s in range(1, ctx_n):
            total = total + buffer[s]
        return total[0:1], total[1:2]

    kt, us = ctx_finish(sums1, ctx_start(sums1, (one_s, one_r), kt, us))
    scale = 1.0 / math.sqrt(gene_count * ctx_n * dp_n)

    def query_pass(start, count, carry):
        at = pl.ds(start, count)
        u = unit[at, :width]
        qf = jnp.exp(feature_scale * u)
        den = head_sum(qf * kt, ones)
        att = head_sum(qf * us, ones, True) / den
        predicted = base_dot[at, 0:1] + jnp.sum(att, axis=1, keepdims=True) * (1.0 / HEAD)
        pred_x[at, :] = jnp.broadcast_to(predicted, (count, 128))
        res = (predicted - target_x[at, 0:1]) * (scale * keep_x[at, 0:1])
        qs = qf * (res / den)
        h = qs * (us - att * kt)
        back = head_sum(h * u, ones) * (1.0 / HEAD)
        rows[at, :width] = (feature_scale * inverse[at, :width] * (h - u * back)).astype(BF16)
        return (
            carry[0] + jnp.sum(qs, axis=0, keepdims=True),
            carry[1] - jnp.sum(qs * att, axis=0, keepdims=True),
        )

    cs, ts = lax.fori_loop(
        0,
        padded // chunk,
        lambda i, carry: query_pass(pl.multiple_of(i * chunk, 16), chunk, carry),
        (none, none),
    )
    cs, ts = query_pass(padded, tok_n, (cs, ts))
    sent = ctx_start(sums2, (two_s, two_r), cs, ts)

    share = width // dp_n

    def core_start(part_grad, grads, recv, sems):
        for j in range(dp_n):
            grads[j] = part_grad[j * share : (j + 1) * share, :]
        return [
            send(
                grads.at[2 * z + 1 - core], recv.at[z], sems, z, z, {"dp": 2 * chip + 1 - core}
            )
            for z in range(chips)
        ]

    def z_start(core_copies, grads, recv, out, into, sems):
        for copy in core_copies:
            copy.wait()
        started = []
        for k in range(1, chips):
            z = lax.rem(chip + k, chips)
            out[k] = (grads[2 * z + core] + recv[z]).astype(BF16)
            started.append(send(out.at[k], into.at[k], sems, k, k, {"dp": 2 * z + core}))
        return grads[2 * chip + core] + recv[chip], started

    def z_finish(total, started, into):
        for copy in started:
            copy.wait()
        for k in range(1, chips):
            total = total + into[k].astype(F32)
        return total

    def outer(lo, hi):
        return lax.dot_general(
            normed[...], rows[:, lo:hi], (((0,), (0,)), ((), ())), preferred_element_type=F32
        )

    copies_q = core_start(outer(0, width), grads_q, core_q, (cq_s, cq_r))
    cs, ts = ctx_finish(sums2, sent)
    pick6 = jnp.where(
        lax.broadcasted_iota(jnp.int32, (width, 128), 0) // HEAD
        == lax.broadcasted_iota(jnp.int32, (width, 128), 1),
        1.0,
        0.0,
    ).astype(BF16)

    def key_pass(start, count):
        at = pl.ds(start, count)
        u = unit[at, width:]
        kf = jnp.exp(feature_scale * u) * keep_x[at, 0:1]
        h = kf * (vwx[at, :] * cs + ts)
        back = head_sum(h * u, ones) * (1.0 / HEAD)
        rows[at, width : 2 * width] = (
            feature_scale * inverse[at, width:] * (h - u * back)
        ).astype(BF16)
        rows[at, 2 * width :] = sum(mm(x, pick6) for x in split(kf * cs)).astype(BF16)

    def key_step(i, carry):
        key_pass(pl.multiple_of(i * chunk, 16), chunk)
        return carry

    steps = padded // chunk
    lax.fori_loop(0, steps // 2, key_step, 0)
    total_q, started_q = z_start(copies_q, grads_q, core_q, zs_q, zr_q, (zq_s, zq_r))
    lax.fori_loop(steps // 2, steps, key_step, 0)
    key_pass(padded, tok_n)
    copies_k = core_start(outer(width, 2 * width + 128), grads_k, core_k, (ck_s, ck_r))
    total_k, started_k = z_start(copies_k, grads_k, core_k, zs_k, zr_k, (zk_s, zk_r))

    hit = gene_lane == idx_col
    tok_pred = pred_x[padded:, 0:1]
    base_row = jnp.transpose(pred_x[0:padded, :])[0:1, :]
    moved = jnp.sum(jnp.where(hit, tok_pred, 0.0), axis=0, keepdims=True)
    final = jnp.where(keep_row > 0.5, base_row, moved)
    pred_ref[...] = final[:, :gene_count]

    total = jnp.concatenate(
        [z_finish(total_q, started_q, zr_q), z_finish(total_k, started_k, zr_k)], axis=1
    )
    span = ctx_recv.shape[2]
    for s in range(ctx_n):
        lo = 256 * min(s, 2)
        part[s] = total[:, lo : lo + span]
    copies = []
    for k in range(1, ctx_n):
        dest = lax.rem(ctx + k, ctx_n)
        copies.append(
            send(part.at[dest], ctx_recv.at[k], (last_s, last_r), k, k, {"ctx": dest})
        )
    for copy in copies:
        copy.wait()
    window = part[ctx]
    for k in range(1, ctx_n):
        window = window + ctx_recv[k]
    tail_part = window[:, 256:]
    head_of = lax.broadcasted_iota(jnp.int32, (1, width), 1) // HEAD
    value_grad = jnp.zeros((share, width), F32)
    for h in range(HEADS):
        value_grad = value_grad + tail_part[:, h : h + 1] * jnp.where(head_of == h, w_row, 0.0)
    result = window[:, 0:288]
    result = jnp.where(ctx == 1, window[:, 32:320], result)
    mixed = jnp.concatenate([window[:, 64:256], value_grad[:, 0:96]], axis=1)
    result = jnp.where(ctx == 2, mixed, result)
    result = jnp.where(ctx == 3, value_grad[:, 96:384], result)
    grad_ref[...] = result


def fused(
    gene_ids,
    counts,
    values,
    lengths,
    bin_edges,
    bin_table,
    value_weight,
    in_weight,
    out_weight,
    gene_table,
    zero_embed,
    qkv_weight,
    proj_weight,
    readout,
    targets,
):
    ctx_n = lax.axis_size("ctx")
    dp_n = lax.axis_size("dp")
    gene_count, width = gene_table.shape
    padded = -(-gene_count // 128) * 128
    tok_n = gene_ids.shape[1]
    chunk = padded // CHUNKS
    total = padded + tok_n
    share = width // dp_n
    vmem = pl.BlockSpec(memory_space=pltpu.VMEM)
    smem = pl.BlockSpec(memory_space=pltpu.SMEM)
    dma = pltpu.SemaphoreType.DMA
    chips = dp_n // 2
    return pl.pallas_call(
        functools.partial(kernel, gene_count, chunk),
        out_shape=(
            jax.ShapeDtypeStruct((1, gene_count), F32),
            jax.ShapeDtypeStruct((share, 3 * width // ctx_n), F32),
        ),
        in_specs=[vmem] * 3 + [smem] * 2 + [vmem] * 10,
        out_specs=(vmem, vmem),
        scratch_shapes=[
            pltpu.VMEM((64, width), F32),
            pltpu.VMEM((256, 256), BF16),
            pltpu.VMEM((width, width), BF16),
            pltpu.VMEM((width, width), BF16),
            pltpu.VMEM((padded, width), F32),
            pltpu.VMEM((1, padded), F32),
            pltpu.VMEM((ctx_n, 8, tok_n), F32),
            pltpu.VMEM((dp_n, 8, tok_n), F32),
            pltpu.VMEM((chips, tok_n, width), BF16),
            pltpu.VMEM((chips, tok_n, width), BF16),
            pltpu.VMEM((chips, tok_n, width), BF16),
            pltpu.VMEM((chips, tok_n, width), BF16),
            pltpu.VMEM((total, width), BF16),
            pltpu.VMEM((total, 2 * width), F32),
            pltpu.VMEM((total, 2 * width), F32),
            pltpu.VMEM((total, width), F32),
            pltpu.VMEM((total, 2 * width + 128), BF16),
            pltpu.VMEM((total, 128), F32),
            pltpu.VMEM((total, 128), F32),
            pltpu.VMEM((total, 128), F32),
            pltpu.VMEM((total, 128), F32),
            pltpu.VMEM((ctx_n, 8, width), F32),
            pltpu.VMEM((ctx_n, 8, width), F32),
            pltpu.VMEM((dp_n, share, width), F32),
            pltpu.VMEM((chips, share, width), F32),
            pltpu.VMEM((chips, share, width), BF16),
            pltpu.VMEM((chips, share, width), BF16),
            pltpu.VMEM((dp_n, share, width + 128), F32),
            pltpu.VMEM((chips, share, width + 128), F32),
            pltpu.VMEM((chips, share, width + 128), BF16),
            pltpu.VMEM((chips, share, width + 128), BF16),
            pltpu.VMEM((ctx_n, share, 384), F32),
            pltpu.VMEM((ctx_n, share, 384), F32),
        ]
        + [dma((n,)) for n in (ctx_n, dp_n, chips, chips, ctx_n, ctx_n, chips, chips, chips, chips, ctx_n) for _ in range(2)],
        compiler_params=pltpu.CompilerParams(
            collective_id=0, has_side_effects=True, vmem_limit_bytes=60 * 2**20
        ),
        cost_estimate=pl.CostEstimate(
            flops=20 * total * width * width, bytes_accessed=6 * 2**20, transcendentals=4 * total * width
        ),
    )(
        gene_ids,
        counts,
        values,
        lengths,
        bin_edges,
        bin_table,
        value_weight,
        in_weight,
        out_weight,
        gene_table,
        zero_embed,
        qkv_weight,
        proj_weight,
        readout,
        targets,
    )


def program(*args):
    ctx_n = lax.axis_size("ctx")
    dp_n = lax.axis_size("dp")
    width = args[9].shape[1]
    fits = ctx_n == 4 and dp_n == 8 and width == 384 and args[0].shape[1] == 128
    fits = fits and args[9].shape[0] <= 2432
    return (fused if fits else body)(*args)


def solution(mesh):
    return jax.shard_map(
        program,
        mesh=mesh,
        in_specs=(
            P("dp", "ctx"),
            P("dp", "ctx"),
            P("dp", "ctx"),
            P("dp"),
            P("dp", None),
            P(),
            P(),
            P(None, "dp"),
            P("dp", None),
            P("ctx", None),
            P(),
            P(),
            P(),
            P(),
            P("dp", "ctx"),
        ),
        out_specs=(P("dp", "ctx"), P("dp", "ctx")),
        check_vma=False,
    )
```
